256 devices in a mesh: doc: 128 (over z, x, y), seq: 2 (over core).
Axes of the slice: x: 4, y: 4, z: 8, core: 2. Of those that a mesh axis runs over, the one named last changes fastest.
Arguments:
- queries: bfloat16 [32768, 4096], P(('doc', 'seq')), may hold values from -6 to 6
- vision: bfloat16 [256, 128, 8192], P(None, 'doc', 'seq'), may hold values from -6 to 6
- key_matrix: bfloat16 [8192, 512], P('seq'), may hold values from -0.0625 to 0.0625
- value_matrix: bfloat16 [8192, 512], P('seq'), may hold values from -0.0625 to 0.0625
- query_gain: float32 [128], replicated, may hold values from 0.5 to 1.5
- key_gain: float32 [128], replicated, may hold values from 0.5 to 1.5
- image_count: int32 [128], P('doc'), may hold values from 1 to 8, as said below
- image_slot: int32 [128, 8], replicated, may hold values from -1 to 255, as said below
- image_pos: int32 [128, 8], P('doc'), may hold values from 0 to 256, as said below
- span_end: int32 [128, 8], P('doc'), may hold values from 1 to 256, as said below
Outputs:
- mixed_rows: bfloat16 [32768, 4096], P(('doc', 'seq'))
The draws below stay inside these ranges and needn't reach their ends.
Inputs may be any that keep to these rules, and one draw needn't show every extreme that they name: `image_count`: the counts sum to 256. For j < image_count[d], image j of document d lies in encoder slot image_slot[d, j]; every slot holds exactly one image; entries with j >= image_count[d] are -1. `image_pos`: non-decreasing in j; 256 for j >= image_count[d]. `span_end`: greater than image_pos for j < image_count[d]; a document's last image is attended to the document's end; 256 for j >= image_count[d].
All inputs are finite; a program needn't handle non-finite values.
Results may differ from the reference program's by a relative error of at most 0.0075.
Values may be sent and summed in bfloat16 or wider, within the bound.
A program may use at most 128 MiB of HBM per device.

```python
import math
import jax
import jax.numpy as jnp
from jax import lax

MODEL_WIDTH = 8192
HEAD_SIZE = 128
QUERY_HEADS = 32
KEY_VALUE_HEADS = 4
IMG_MAX = 8
TEXT_LENGTH = 256
TOKENS = 32768
ENC_SLOTS = 256
VISION_ROWS = 128
N_DOC = 128


def image_layout(key):
    blocks = N_DOC // 8
    key_first, key_other, key_last, key_perm, key_pos, key_end = jax.random.split(key, 6)
    first_targets = jax.random.randint(key_first, (blocks, 7), 0, 8)
    block_ids = jnp.arange(blocks, dtype=jnp.int32)[:, None]
    first_targets = jnp.where(block_ids == 0, first_targets[:, :1], first_targets)
    uniform_block = jnp.all(first_targets == first_targets[:, :1], axis=1)
    other_target = (first_targets[:, 0] + 1 + jax.random.randint(key_other, (blocks,), 0, 7)) % 8
    anywhere = jax.random.randint(key_last, (blocks,), 0, 8)
    last_target = jnp.where(uniform_block, other_target, anywhere)
    targets = jnp.concatenate([first_targets, last_target[:, None]], axis=1)
    eight_ids = jnp.arange(8, dtype=jnp.int32)
    extras = jnp.sum((targets[:, :, None] == eight_ids[None, None, :]).astype(jnp.int32), axis=1)
    counts = (1 + extras).reshape(N_DOC).astype(jnp.int32)
    starts = jnp.cumsum(counts) - counts
    slot_ids = jnp.arange(IMG_MAX, dtype=jnp.int32)[None, :]
    present = slot_ids < counts[:, None]
    slot_order = jax.random.permutation(key_perm, ENC_SLOTS).astype(jnp.int32)
    global_ids = jnp.minimum(starts[:, None] + slot_ids, ENC_SLOTS - 1)
    slot_table = jnp.where(present, slot_order[global_ids], -1).astype(jnp.int32)
    raw_positions = jax.random.randint(key_pos, (N_DOC, IMG_MAX), 0, TEXT_LENGTH)
    raw_positions = jnp.where(present, raw_positions, TEXT_LENGTH)
    positions = jnp.sort(raw_positions, axis=1)
    first_doc = (jnp.arange(N_DOC, dtype=jnp.int32)[:, None] == 0) & (slot_ids == 0)
    positions = jnp.where(first_doc, 0, positions).astype(jnp.int32)
    span_reach = jax.random.randint(key_end, (N_DOC, IMG_MAX), 0, jnp.maximum(TEXT_LENGTH - positions, 1))
    span_ends = positions + 1 + span_reach
    last_image = slot_ids == counts[:, None] - 1
    span_ends = jnp.where(last_image, TEXT_LENGTH, span_ends)
    span_ends = jnp.where(present, span_ends, TEXT_LENGTH).astype(jnp.int32)
    return (counts, slot_table, positions, span_ends)


def draw_image_count(key, part):
    layout = image_layout(key)
    return layout[0]


def draw_image_slot(key, part):
    layout = image_layout(key)
    return layout[1]


def draw_image_pos(key, part):
    layout = image_layout(key)
    return layout[2]


def draw_span_end(key, part):
    layout = image_layout(key)
    return layout[3]


def level_of(stream_key, shape, cuts, low, top_value):
    loudness, own = 1.0, jax.random.fold_in(stream_key, 6)
    for position, shards_of in cuts:
        draws = jnp.exp(jax.random.uniform(jax.random.fold_in(own, position), (shards_of,), jnp.float32, low / len(cuts), top_value / len(cuts)))
        loudness = loudness * jnp.repeat(draws, shape[position] // shards_of).reshape([-1 if axis == position else 1 for axis in range(len(shape))])
    return loudness


def noise(key, dims, spread, bound, pieces=(), held_as=jnp.bfloat16):
    entries = jax.random.normal(key, dims, jnp.float32) * spread
    if len(pieces) > 0:
        entries = level_of(key, dims, pieces, -0.22, 0.18) * entries
    return jnp.clip(entries, min=-bound, max=bound).astype(held_as)


def setup_inputs(seed: int = 0) -> dict:
    arg_keys = jax.random.split(jax.random.key(seed), 11)
    return {
        "queries": noise(arg_keys[0], (TOKENS, QUERY_HEADS * HEAD_SIZE), 1.0, 6.0, ((0, 256),)),
        "vision": noise(arg_keys[1], (ENC_SLOTS, VISION_ROWS, MODEL_WIDTH), 1.0, 6.0, ((1, 128), (2, 2))),
        "key_matrix": noise(arg_keys[2], (MODEL_WIDTH, KEY_VALUE_HEADS * HEAD_SIZE), MODEL_WIDTH ** -0.5, 0.0625, ((0, 2),)),
        "value_matrix": noise(arg_keys[3], (MODEL_WIDTH, KEY_VALUE_HEADS * HEAD_SIZE), MODEL_WIDTH ** -0.5, 0.0625, ((0, 2),)),
        "query_gain": jnp.clip(1.0 + 0.1 * jax.random.normal(arg_keys[4], (HEAD_SIZE,), jnp.float32), 0.5, 1.5),
        "key_gain": jnp.clip(1.0 + 0.1 * jax.random.normal(arg_keys[5], (HEAD_SIZE,), jnp.float32), 0.5, 1.5),
        "image_count": draw_image_count(jax.random.fold_in(arg_keys[10], 71), 0),
        "image_slot": draw_image_slot(jax.random.fold_in(arg_keys[10], 71), 0),
        "image_pos": draw_image_pos(jax.random.fold_in(arg_keys[10], 71), 0),
        "span_end": draw_span_end(jax.random.fold_in(arg_keys[10], 71), 0),
    }


epsilon = 1e-05

def head_norm(values, scales):
    mean_square = lax.optimization_barrier(jnp.mean(values * values, axis=-1, keepdims=True))
    return values * lax.rsqrt(mean_square + epsilon) * scales

def reference(queries, vision, key_matrix, value_matrix, query_gain, key_gain, image_count, image_slot, image_pos, span_end):

    def encode(picture_rows):
        key_portion = jnp.dot(picture_rows, key_matrix, preferred_element_type=jnp.float32).reshape(VISION_ROWS, KEY_VALUE_HEADS, HEAD_SIZE)
        value_portion = jnp.dot(picture_rows, value_matrix, preferred_element_type=jnp.float32).reshape(VISION_ROWS, KEY_VALUE_HEADS, HEAD_SIZE)
        normed = head_norm(key_portion, key_gain).astype(jnp.bfloat16)
        return jnp.stack([normed, value_portion.astype(jnp.bfloat16)], axis=2)
    encoded = lax.map(encode, vision)
    query_head_rows = queries.astype(jnp.float32).reshape(N_DOC, TEXT_LENGTH, KEY_VALUE_HEADS, QUERY_HEADS // KEY_VALUE_HEADS, HEAD_SIZE)
    normed_queries = head_norm(query_head_rows, query_gain).astype(jnp.bfloat16)
    positions = jnp.arange(TEXT_LENGTH, dtype=jnp.int32)
    slots_seen = jnp.arange(IMG_MAX, dtype=jnp.int32)
    score_scale = 1.0 / math.sqrt(HEAD_SIZE)

    def attend(inputs):
        doc_queries, doc_slots, doc_count, doc_pos, doc_end = inputs
        picked = jnp.take(encoded, jnp.maximum(doc_slots, 0).astype(jnp.int32), axis=0)
        key_portion = picked[:, :, :, 0].astype(jnp.float32)
        value_portion = picked[:, :, :, 1].astype(jnp.float32)
        attends = (slots_seen[None, :] < doc_count) & (doc_pos[None, :] <= positions[:, None]) & (positions[:, None] < doc_end[None, :])
        scores = jnp.einsum('tkgd,jvkd->tkgjv', doc_queries.astype(jnp.float32), key_portion) * score_scale
        weights = jnp.where(attends[:, None, None, :, None], jnp.exp(scores), 0.0).astype(jnp.bfloat16)
        numerator = jnp.einsum('tkgjv,jvkd->tkgd', weights.astype(jnp.float32), value_portion)
        denominator = lax.optimization_barrier(jnp.sum(weights.astype(jnp.float32), axis=(3, 4)))
        reached = jnp.any(attends, axis=1)[:, None, None]
        quotient = numerator / jnp.where(reached, denominator, 1.0)[..., None]
        return jnp.where(reached[..., None], quotient, 0.0).astype(jnp.bfloat16)
    mixed_rows = lax.map(attend, (normed_queries, image_slot, image_count, image_pos, span_end))
    return mixed_rows.reshape(TOKENS, QUERY_HEADS * HEAD_SIZE)
```

```python
import math

import jax
import jax.numpy as jnp
from jax import lax
from jax.sharding import PartitionSpec as P

HEAD_SIZE = 128
QUERY_HEADS = 32
KEY_VALUE_HEADS = 4
IMG_MAX = 8


epsilon = 1e-05


def head_norm(values, scales):
    mean_square = jnp.mean(values * values, axis=-1, keepdims=True)
    return values * lax.rsqrt(mean_square + epsilon) * scales


def shards(
    queries,
    vision,
    key_matrix,
    value_matrix,
    query_gain,
    key_gain,
    image_count,
    image_slot,
    image_pos,
    span_end,
):
    n_slots = vision.shape[0]
    core = lax.axis_index("seq")
    rows = vision.reshape(n_slots, -1)
    keys = jnp.dot(rows, key_matrix, preferred_element_type=jnp.float32)
    values = jnp.dot(rows, value_matrix, preferred_element_type=jnp.float32)
    half = keys.shape[1] // 2
    other = [(0, 1), (1, 0)]

    def pick(c):
        start = c * half
        return jnp.concatenate(
            [lax.dynamic_slice_in_dim(keys, start, half, 1), lax.dynamic_slice_in_dim(values, start, half, 1)], axis=1
        )

    mine = pick(core) + lax.ppermute(pick(1 - core), "seq", other)
    mine = mine.reshape(n_slots, 2, 2, HEAD_SIZE)
    kv = jnp.concatenate(
        [head_norm(mine[:, 0], key_gain).astype(jnp.bfloat16), mine[:, 1].astype(jnp.bfloat16)], axis=1
    ).reshape(n_slots, 4 * HEAD_SIZE)
    slots = image_slot.reshape(-1)
    one_hot = (slots[:, None] == jnp.arange(n_slots, dtype=jnp.int32)[None, :]).astype(jnp.bfloat16)
    packed = jnp.dot(one_hot, kv, preferred_element_type=jnp.float32).astype(jnp.bfloat16)
    packed = packed.reshape(image_slot.shape[0], IMG_MAX * 4 * HEAD_SIZE)
    got = lax.all_to_all(packed, "doc", split_axis=0, concat_axis=0, tiled=True)
    theirs = lax.ppermute(got, "seq", other)
    first = jnp.where(core == 0, got, theirs).reshape(-1, IMG_MAX, 2, 2, HEAD_SIZE)
    second = jnp.where(core == 0, theirs, got).reshape(-1, IMG_MAX, 2, 2, HEAD_SIZE)
    both = jnp.concatenate([first, second], axis=3)
    n_keys = both.shape[0] * IMG_MAX
    both = both.reshape(n_keys, 2, KEY_VALUE_HEADS, HEAD_SIZE)
    local_tokens = queries.shape[0]
    positions = core * local_tokens + jnp.arange(local_tokens, dtype=jnp.int32)
    q = queries.astype(jnp.float32).reshape(local_tokens, KEY_VALUE_HEADS, QUERY_HEADS // KEY_VALUE_HEADS, HEAD_SIZE)
    q = head_norm(q, query_gain).astype(jnp.bfloat16)
    seen = jnp.arange(IMG_MAX, dtype=jnp.int32)
    attends = (
        (seen[None, :] < image_count[0])
        & (image_pos[0][None, :] <= positions[:, None])
        & (positions[:, None] < span_end[0][None, :])
    )
    scores = jnp.einsum("tkgd,nkd->tkgn", q, both[:, 0], preferred_element_type=jnp.float32)
    scores = scores * (1.0 / math.sqrt(HEAD_SIZE))
    key_mask = jnp.tile(attends, (1, n_keys // IMG_MAX))
    weights = jnp.where(key_mask[:, None, None, :], jnp.exp(scores), 0.0).astype(jnp.bfloat16)
    numerator = jnp.einsum("tkgn,nkd->tkgd", weights, both[:, 1], preferred_element_type=jnp.float32)
    denominator = jnp.sum(weights, axis=3, dtype=jnp.float32)
    reached = jnp.any(attends, axis=1)[:, None, None]
    quotient = numerator / jnp.where(reached, denominator, 1.0)[..., None]
    mixed_rows = jnp.where(reached[..., None], quotient, 0.0).astype(jnp.bfloat16)
    return mixed_rows.reshape(local_tokens, QUERY_HEADS * HEAD_SIZE)


def solution(mesh):
    in_specs = (
        P(("doc", "seq"), None),
        P(None, "doc", "seq"),
        P("seq", None),
        P("seq", None),
        P(),
        P(),
        P("doc"),
        P(),
        P("doc", None),
        P("doc", None),
    )
    out_specs = P(("doc", "seq"), None)
    return jax.shard_map(shards, mesh=mesh, in_specs=in_specs, out_specs=out_specs, check_vma=False)
```

```python
import functools
import math

import jax
import jax.numpy as jnp
from jax import lax
from jax.experimental import pallas as pl
from jax.experimental.pallas import tpu as pltpu
from jax.sharding import PartitionSpec as P

HEAD_SIZE = 128
QUERY_HEADS = 32
KEY_VALUE_HEADS = 4
IMG_MAX = 8
GROUP = QUERY_HEADS // KEY_VALUE_HEADS
PLANE = 16
PLANES = 8
CAPACITY = 48
MESH = pl.DeviceIdType.MESH
MASKED = -32768.0

epsilon = 1e-05


def head_norm(values, scales):
    mean_square = jnp.mean(values * values, axis=-1, keepdims=True)
    return values * lax.rsqrt(mean_square + epsilon) * scales


def general_route(
    queries,
    vision,
    key_matrix,
    value_matrix,
    query_gain,
    key_gain,
    image_count,
    image_slot,
    image_pos,
    span_end,
):
    n_slots = vision.shape[0]
    core = lax.axis_index("seq")
    rows = vision.reshape(n_slots, -1)
    keys = jnp.dot(rows, key_matrix, preferred_element_type=jnp.float32)
    values = jnp.dot(rows, value_matrix, preferred_element_type=jnp.float32)
    half = keys.shape[1] // 2
    other = [(0, 1), (1, 0)]

    def pick(c):
        start = c * half
        return jnp.concatenate(
            [lax.dynamic_slice_in_dim(keys, start, half, 1), lax.dynamic_slice_in_dim(values, start, half, 1)], axis=1
        )

    mine = pick(core) + lax.ppermute(pick(1 - core), "seq", other)
    mine = mine.reshape(n_slots, 2, 2, HEAD_SIZE)
    kv = jnp.concatenate(
        [head_norm(mine[:, 0], key_gain).astype(jnp.bfloat16), mine[:, 1].astype(jnp.bfloat16)], axis=1
    ).reshape(n_slots, 4 * HEAD_SIZE)
    slots = image_slot.reshape(-1)
    one_hot = (slots[:, None] == jnp.arange(n_slots, dtype=jnp.int32)[None, :]).astype(jnp.bfloat16)
    packed = jnp.dot(one_hot, kv, preferred_element_type=jnp.float32).astype(jnp.bfloat16)
    packed = packed.reshape(image_slot.shape[0], IMG_MAX * 4 * HEAD_SIZE)
    got = lax.all_to_all(packed, "doc", split_axis=0, concat_axis=0, tiled=True)
    theirs = lax.ppermute(got, "seq", other)
    first = jnp.where(core == 0, got, theirs).reshape(-1, IMG_MAX, 2, 2, HEAD_SIZE)
    second = jnp.where(core == 0, theirs, got).reshape(-1, IMG_MAX, 2, 2, HEAD_SIZE)
    both = jnp.concatenate([first, second], axis=3)
    n_keys = both.shape[0] * IMG_MAX
    both = both.reshape(n_keys, 2, KEY_VALUE_HEADS, HEAD_SIZE)
    local_tokens = queries.shape[0]
    positions = core * local_tokens + jnp.arange(local_tokens, dtype=jnp.int32)
    q = queries.astype(jnp.float32).reshape(local_tokens, KEY_VALUE_HEADS, GROUP, HEAD_SIZE)
    q = head_norm(q, query_gain).astype(jnp.bfloat16)
    seen = jnp.arange(IMG_MAX, dtype=jnp.int32)
    attends = (
        (seen[None, :] < image_count[0])
        & (image_pos[0][None, :] <= positions[:, None])
        & (positions[:, None] < span_end[0][None, :])
    )
    scores = jnp.einsum("tkgd,nkd->tkgn", q, both[:, 0], preferred_element_type=jnp.float32)
    scores = scores * (1.0 / math.sqrt(HEAD_SIZE))
    key_mask = jnp.tile(attends, (1, n_keys // IMG_MAX))
    weights = jnp.where(key_mask[:, None, None, :], jnp.exp(scores), 0.0).astype(jnp.bfloat16)
    numerator = jnp.einsum("tkgn,nkd->tkgd", weights, both[:, 1], preferred_element_type=jnp.float32)
    denominator = jnp.sum(weights, axis=3, dtype=jnp.float32)
    reached = jnp.any(attends, axis=1)[:, None, None]
    quotient = numerator / jnp.where(reached, denominator, 1.0)[..., None]
    mixed_rows = jnp.where(reached[..., None], quotient, 0.0).astype(jnp.bfloat16)
    return mixed_rows.reshape(local_tokens, QUERY_HEADS * HEAD_SIZE)


def iota(shape, axis):
    return lax.broadcasted_iota(jnp.int32, shape, axis)


def flag(condition):
    return condition.astype(jnp.float32).astype(jnp.bfloat16)


def mm(a, b, contract=((1,), (0,))):
    return lax.dot_general(a, b, (contract, ((), ())), preferred_element_type=jnp.float32)


RIGHT = ((1,), (1,))


def fused_kernel(
    q_hbm,
    x_hbm,
    wk_hbm,
    wv_hbm,
    qg_ref,
    kg_ref,
    count_ref,
    slot_ref,
    pos_ref,
    end_ref,
    out_hbm,
    q_v,
    x_v,
    w_v,
    part_send,
    part_recv,
    part_mine,
    pick1,
    expand,
    send1,
    recv1,
    send2,
    recv2,
    q_send,
    q_all,
    k_tail,
    o_v,
    o_send,
    local_sem,
    w_sem,
    out_sem,
    part_sems,
    q_sems,
    o_sems,
    s1_sem,
    r1_sem,
    s2_sem,
    r2_sem,
):
    doc = lax.axis_index("doc")
    core = lax.axis_index("seq")
    sibling = 1 - core
    z, p = doc // PLANE, doc % PLANE
    px, py = p // 4, p % 4
    tokens = q_v.shape[0]
    n_slots = x_v.shape[0]
    depth = x_v.shape[1]
    piece = depth // 4

    q_copy = pltpu.make_async_copy(q_hbm, q_v, local_sem.at[0])
    q_copy.start()

    def x_copy(c):
        cols = pl.ds(c * piece, piece)
        return pltpu.make_async_copy(x_hbm.at[:, cols], x_v.at[:, cols], local_sem.at[1 + c])

    def w_copies(h, t, c):
        owner = core if t == 0 else sibling
        head = pl.ds(pl.multiple_of((owner * 2 + h) * HEAD_SIZE, HEAD_SIZE), HEAD_SIZE)
        rows = pl.ds(c * piece, piece)
        slot = h * 2 + t
        return [
            pltpu.make_async_copy(
                src.at[rows, head],
                w_v.at[slot, rows, pl.ds(i * HEAD_SIZE, HEAD_SIZE)],
                w_sem.at[slot, c, i],
            )
            for i, src in enumerate((wk_hbm, wv_hbm))
        ]

    for c in range(4):
        x_copy(c).start()
        for copy in w_copies(0, 1, c):
            copy.start()
    for h, t in ((0, 0), (1, 1), (1, 0)):
        for c in range(4):
            for copy in w_copies(h, t, c):
                copy.start()

    def z_to(step):
        return (z + step) % PLANES

    def plane_to(step):
        return ((px + step // 4) % 4) * 4 + (py + step % 4) % 4

    def plane_from(step):
        return ((px + 4 - step // 4) % 4) * 4 + (py + 4 - step % 4) % 4

    barrier = pltpu.get_barrier_semaphore()
    pl.semaphore_signal(barrier, inc=1, device_id=(doc, sibling), device_id_type=MESH)

    def greet_z(i, carry):
        pl.semaphore_signal(barrier, inc=1, device_id=(z_to(i) * PLANE + p, core), device_id_type=MESH)
        return carry

    def greet_plane(i, carry):
        pl.semaphore_signal(barrier, inc=1, device_id=(z * PLANE + plane_to(i), core), device_id_type=MESH)
        return carry

    lax.fori_loop(1, PLANES, greet_z, 0)
    lax.fori_loop(1, PLANE, greet_plane, 0)

    slots_t = slot_ref[...]
    present = slots_t >= 0
    there = flag(present)
    d_row, d_col = iota((128, 128), 0), iota((128, 128), 1)
    same = (d_row // PLANE) == (d_col // PLANE)
    before = mm(there, flag(same & (d_row < d_col)))
    totals = mm(there, flag(same)).astype(jnp.bfloat16)
    earlier = mm(flag(iota((8, 8), 1) < iota((8, 8), 0)), totals)
    rank = before + earlier
    identity = flag(d_row == d_col)
    slot_cols = mm(identity, slots_t.astype(jnp.float32).astype(jnp.bfloat16), RIGHT)
    rank_cols = mm(identity, jnp.where(present, rank, 0.0).astype(jnp.bfloat16), RIGHT)
    plane_base = (CAPACITY * (iota((128, 1), 0) // PLANE)).astype(jnp.float32) + 1.0
    slot_lane = iota((1, n_slots), 1).astype(jnp.float32)
    found = jnp.zeros((128, n_slots), jnp.float32)
    for j in range(IMG_MAX):
        found = found + jnp.where(
            slot_cols[:, j : j + 1] == slot_lane, rank_cols[:, j : j + 1] + plane_base, 0.0
        )
    goes_to = jnp.sum(found, axis=0, keepdims=True) - 1.0
    pick1[...] = flag(iota((PLANES * CAPACITY, n_slots), 0).astype(jnp.float32) == goes_to)

    rows_e, cols_e = 4 * PLANE * IMG_MAX, 4 * CAPACITY
    mine_doc = flag(iota((rows_e, 128), 1) == z * PLANE + iota((rows_e, 128), 0) // (4 * IMG_MAX))
    rank_plus = jnp.where(present, rank + 1.0, 0.0).astype(jnp.bfloat16)
    by_slot = mm(mine_doc, rank_plus, RIGHT)
    chosen = iota((rows_e, IMG_MAX), 1) == iota((rows_e, IMG_MAX), 0) % IMG_MAX
    row_rank = jnp.sum(jnp.where(chosen, by_slot, 0.0), axis=1, keepdims=True)
    source = (iota((rows_e, 1), 0) // IMG_MAX) % 4
    row_target = jnp.where(row_rank > 0.0, row_rank - 1.0 + (CAPACITY * source).astype(jnp.float32), -1.0)
    expand[...] = flag(iota((rows_e, cols_e), 1).astype(jnp.float32) == row_target)

    lane = iota((1, HEAD_SIZE), 1)
    first_t = jnp.zeros((1, HEAD_SIZE), jnp.int32)
    last_t = jnp.zeros((1, HEAD_SIZE), jnp.int32)
    for j in range(IMG_MAX):
        first_t = jnp.where(lane == j, pos_ref[0, j], first_t)
        last_t = jnp.where(lane == j, end_ref[0, j], last_t)
    block = iota((2 * tokens, HEAD_SIZE), 0) // tokens
    owner = jnp.where(block == 0, core, sibling)
    t_pos = owner * tokens + iota((2 * tokens, HEAD_SIZE), 0) % tokens
    attends = (lane < count_ref[0]) & (first_t <= t_pos) & (t_pos < last_t)
    q_tail = flag(jnp.logical_not(attends))
    n_keys = k_tail.shape[0]
    k_tail[...] = jnp.where(
        iota((n_keys, HEAD_SIZE), 1) == iota((n_keys, HEAD_SIZE), 0) % IMG_MAX, MASKED, 0.0
    ).astype(jnp.bfloat16)

    q_copy.wait()
    q_gain = qg_ref[...]
    half_width = QUERY_HEADS // 2 * HEAD_SIZE

    def norm_queries(i, carry):
        at = pl.multiple_of(i * HEAD_SIZE, HEAD_SIZE)
        own_cols = pl.ds(pl.multiple_of(core * half_width + at, HEAD_SIZE), HEAD_SIZE)
        sib_cols = pl.ds(pl.multiple_of(sibling * half_width + at, HEAD_SIZE), HEAD_SIZE)
        q_all[0, :, pl.ds(at, HEAD_SIZE)] = head_norm(q_v[:, own_cols].astype(jnp.float32), q_gain).astype(jnp.bfloat16)
        q_send[:, pl.ds(at, HEAD_SIZE)] = head_norm(q_v[:, sib_cols].astype(jnp.float32), q_gain).astype(jnp.bfloat16)
        return carry

    lax.fori_loop(0, QUERY_HEADS // 2, norm_queries, 0)

    def project(h, t):
        total = None
        for c in range(4):
            if (h, t) == (0, 1):
                x_copy(c).wait()
            for copy in w_copies(h, t, c):
                copy.wait()
            rows = pl.ds(c * piece, piece)
            term = mm(x_v[:, rows], w_v[h * 2 + t, rows, :])
            total = term if total is None else total + term
        return total

    def part_copy(h):
        return pltpu.make_async_remote_copy(
            src_ref=part_send.at[h],
            dst_ref=part_recv.at[h],
            send_sem=part_sems.at[0, h],
            recv_sem=part_sems.at[1, h],
            device_id=(doc, sibling),
            device_id_type=MESH,
        )

    q_exchange = pltpu.make_async_remote_copy(
        src_ref=q_send,
        dst_ref=q_all.at[1],
        send_sem=q_sems.at[0],
        recv_sem=q_sems.at[1],
        device_id=(doc, sibling),
        device_id_type=MESH,
    )

    def hop1(h, i):
        return pltpu.make_async_remote_copy(
            src_ref=send1.at[h, z_to(i)],
            dst_ref=recv1.at[h, z],
            send_sem=s1_sem.at[h, i - 1],
            recv_sem=r1_sem.at[h, i - 1],
            device_id=(z_to(i) * PLANE + p, core),
            device_id_type=MESH,
        )

    def hop1_in(h, i):
        source = z_to(PLANES - i)
        return pltpu.make_async_remote_copy(
            src_ref=send1.at[h, source],
            dst_ref=recv1.at[h, source],
            send_sem=s1_sem.at[h, i - 1],
            recv_sem=r1_sem.at[h, i - 1],
            device_id=(source * PLANE + p, core),
            device_id_type=MESH,
        )

    def hop2(h, i):
        return pltpu.make_async_remote_copy(
            src_ref=send2.at[h, plane_to(i)],
            dst_ref=recv2.at[h, p],
            send_sem=s2_sem.at[h, i - 1],
            recv_sem=r2_sem.at[h, i - 1],
            device_id=(z * PLANE + plane_to(i), core),
            device_id_type=MESH,
        )

    def hop2_in(h, i):
        source = plane_from(i)
        return pltpu.make_async_remote_copy(
            src_ref=send2.at[h, source],
            dst_ref=recv2.at[h, source],
            send_sem=s2_sem.at[h, i - 1],
            recv_sem=r2_sem.at[h, i - 1],
            device_id=(z * PLANE + source, core),
            device_id_type=MESH,
        )

    def each(low, high, act):
        def body(i, carry):
            act(i)
            return carry

        lax.fori_loop(low, high, body, 0)

    key_gain = kg_ref[...]

    def encode_and_pack(h):
        part_copy(h).wait_recv()
        total = part_mine[...] + part_recv[h]
        keys = head_norm(total[:, :HEAD_SIZE], key_gain).astype(jnp.bfloat16)
        values = total[:, HEAD_SIZE:].astype(jnp.bfloat16)
        kv = jnp.concatenate([keys, values], axis=1)
        packed = mm(pick1[...], kv).astype(jnp.bfloat16)
        send1[h] = packed.reshape(PLANES, CAPACITY, 2 * HEAD_SIZE)
        each(1, PLANES, lambda i: hop1(h, i).start())
        recv1[h, z] = send1[h, z]

    part_send[0] = project(0, 1)
    pl.semaphore_wait(barrier, PLANES - 1 + PLANE - 1 + 1)
    part_copy(0).start()
    part_mine[...] = project(0, 0)
    part_send[1] = project(1, 1)
    part_copy(1).start()
    encode_and_pack(0)
    q_exchange.start()
    part_mine[...] = project(1, 0)
    encode_and_pack(1)

    def expand_and_send(h):
        each(1, PLANES, lambda i: hop1_in(h, i).wait_recv())
        for s in range(2):
            packed = recv1[h, pl.ds(4 * s, 4)].reshape(4 * CAPACITY, 2 * HEAD_SIZE)
            rows = mm(expand[...], packed).astype(jnp.bfloat16)
            send2[h, :, pl.ds(4 * IMG_MAX * s, 4 * IMG_MAX), :] = rows.reshape(PLANE, 4 * IMG_MAX, 2 * HEAD_SIZE)
        each(1, PLANE, lambda i: hop2(h, i).start())
        recv2[h, p] = send2[h, p]

    expand_and_send(0)
    expand_and_send(1)
    q_exchange.wait_recv()

    ones = jnp.ones((n_keys, HEAD_SIZE), jnp.bfloat16)
    scale = 1.0 / math.sqrt(HEAD_SIZE)

    def o_copy(h):
        return pltpu.make_async_remote_copy(
            src_ref=o_send.at[h],
            dst_ref=o_v.at[core * 2 + h],
            send_sem=o_sems.at[0, h],
            recv_sem=o_sems.at[1, h],
            device_id=(doc, sibling),
            device_id_type=MESH,
        )

    def o_in(h):
        return pltpu.make_async_remote_copy(
            src_ref=o_send.at[h],
            dst_ref=o_v.at[sibling * 2 + h],
            send_sem=o_sems.at[0, h],
            recv_sem=o_sems.at[1, h],
            device_id=(doc, sibling),
            device_id_type=MESH,
        )

    def out_copy(head, i):
        return pltpu.make_async_copy(o_v.at[head], out_hbm.at[head], out_sem.at[i])

    def attend(h):
        each(1, PLANE, lambda i: hop2_in(h, i).wait_recv())
        kv = recv2[h].reshape(n_keys, 2 * HEAD_SIZE)
        keys = jnp.concatenate([kv[:, :HEAD_SIZE], k_tail[...]], axis=1)
        values = jnp.concatenate([kv[:, HEAD_SIZE:], ones], axis=1)

        def head(g, carry):
            at = pl.multiple_of((h * GROUP + g) * HEAD_SIZE, HEAD_SIZE)
            q = q_all[:, :, pl.ds(at, HEAD_SIZE)].reshape(2 * tokens, HEAD_SIZE)
            scores = mm(jnp.concatenate([q, q_tail], axis=1), keys, RIGHT)
            weights = jnp.exp(scores * scale).astype(jnp.bfloat16)
            mixed = mm(weights, values)
            total = mixed[:, HEAD_SIZE:]
            out = (mixed[:, :HEAD_SIZE] / jnp.where(total > 0.0, total, 1.0)).astype(jnp.bfloat16)
            cols = pl.ds(pl.multiple_of(g * HEAD_SIZE, HEAD_SIZE), HEAD_SIZE)
            o_v[core * 2 + h, :, cols] = out[:tokens]
            o_send[h, :, cols] = out[tokens:]
            return carry

        lax.fori_loop(0, GROUP, head, 0)
        o_copy(h).start()
        out_copy(core * 2 + h, h).start()

    attend(0)
    attend(1)
    for h in range(2):
        o_in(h).wait_recv()
        out_copy(sibling * 2 + h, 2 + h).start()
    for h in range(2):
        part_copy(h).wait_send()
        each(1, PLANES, lambda i: hop1(h, i).wait_send())
        each(1, PLANE, lambda i: hop2(h, i).wait_send())
        o_copy(h).wait_send()
    q_exchange.wait_send()
    for h in range(2):
        out_copy(core * 2 + h, h).wait()
        out_copy(sibling * 2 + h, 2 + h).wait()


def packed_route(
    queries,
    vision,
    key_matrix,
    value_matrix,
    query_gain,
    key_gain,
    image_count,
    image_slot,
    image_pos,
    span_end,
):
    tokens, width = queries.shape
    n_slots = vision.shape[0]
    depth = vision.shape[2]
    two = 2 * HEAD_SIZE
    anywhere = pl.BlockSpec(memory_space=pl.ANY)
    vmem = pl.BlockSpec(memory_space=pltpu.VMEM)
    smem = pl.BlockSpec(memory_space=pltpu.SMEM)
    bf16, f32 = jnp.bfloat16, jnp.float32
    dma = pltpu.SemaphoreType.DMA
    out = pl.pallas_call(
        fused_kernel,
        out_shape=jax.ShapeDtypeStruct((KEY_VALUE_HEADS, tokens, GROUP * HEAD_SIZE), bf16),
        in_specs=[anywhere, anywhere, anywhere, anywhere, vmem, vmem, smem, vmem, smem, smem],
        out_specs=anywhere,
        scratch_shapes=[
            pltpu.VMEM((tokens, width), bf16),
            pltpu.VMEM((n_slots, depth), bf16),
            pltpu.VMEM((4, depth, two), bf16),
            pltpu.VMEM((2, n_slots, two), f32),
            pltpu.VMEM((2, n_slots, two), f32),
            pltpu.VMEM((n_slots, two), f32),
            pltpu.VMEM((PLANES * CAPACITY, n_slots), bf16),
            pltpu.VMEM((4 * PLANE * IMG_MAX, 4 * CAPACITY), bf16),
            pltpu.VMEM((2, PLANES, CAPACITY, two), bf16),
            pltpu.VMEM((2, PLANES, CAPACITY, two), bf16),
            pltpu.VMEM((2, PLANE, PLANES * IMG_MAX, two), bf16),
            pltpu.VMEM((2, PLANE, PLANES * IMG_MAX, two), bf16),
            pltpu.VMEM((tokens, width // 2), bf16),
            pltpu.VMEM((2, tokens, width // 2), bf16),
            pltpu.VMEM((PLANE * PLANES * IMG_MAX, HEAD_SIZE), bf16),
            pltpu.VMEM((KEY_VALUE_HEADS, tokens, GROUP * HEAD_SIZE), bf16),
            pltpu.VMEM((2, tokens, GROUP * HEAD_SIZE), bf16),
            dma((5,)),
            dma((4, 4, 2)),
            dma((4,)),
            dma((2, 2)),
            dma((2,)),
            dma((2, 2)),
            dma((2, PLANES - 1)),
            dma((2, PLANES - 1)),
            dma((2, PLANE - 1)),
            dma((2, PLANE - 1)),
        ],
        compiler_params=pltpu.CompilerParams(
            collective_id=0, has_side_effects=True, vmem_limit_bytes=48 * 1024 * 1024
        ),
        name="fused_cross_attention",
    )(
        queries,
        vision.reshape(n_slots, depth),
        key_matrix,
        value_matrix,
        query_gain.reshape(1, HEAD_SIZE),
        key_gain.reshape(1, HEAD_SIZE),
        image_count,
        image_slot.T,
        image_pos,
        span_end,
    )
    return out.transpose(1, 0, 2).reshape(tokens, width)


def shards(*arrays):
    image_slot = arrays[7]
    per_plane = jnp.sum((image_slot >= 0).reshape(PLANES, -1).astype(jnp.int32), axis=1)
    return lax.cond(jnp.max(per_plane) <= CAPACITY, packed_route, general_route, *arrays)


def solution(mesh):
    in_specs = (
        P(("doc", "seq"), None),
        P(None, "doc", "seq"),
        P("seq", None),
        P("seq", None),
        P(),
        P(),
        P("doc"),
        P(),
        P("doc", None),
        P("doc", None),
    )
    out_specs = P(("doc", "seq"), None)
    return jax.shard_map(shards, mesh=mesh, in_specs=in_specs, out_specs=out_specs, check_vma=False)
```

```python
import functools
import math

import jax
import jax.numpy as jnp
from jax import lax
from jax.experimental import pallas as pl
from jax.experimental.pallas import tpu as pltpu
from jax.sharding import PartitionSpec as P

HEAD_SIZE = 128
QUERY_HEADS = 32
KEY_VALUE_HEADS = 4
IMG_MAX = 8
GROUP = QUERY_HEADS // KEY_VALUE_HEADS
PLANE = 16
PLANES = 8
CAPACITY = 48
MESH = pl.DeviceIdType.MESH
MASKED = -32768.0
PIECES = 8
UNROLL = 4
Z_STEPS = (0, 1, 7, 2, 6, 3, 5, 4)

epsilon = 1e-05


def head_norm(values, scales):
    mean_square = jnp.mean(values * values, axis=-1, keepdims=True)
    return values * lax.rsqrt(mean_square + epsilon) * scales


def general_route(
    queries,
    vision,
    key_matrix,
    value_matrix,
    query_gain,
    key_gain,
    image_count,
    image_slot,
    image_pos,
    span_end,
):
    n_slots = vision.shape[0]
    core = lax.axis_index("seq")
    rows = vision.reshape(n_slots, -1)
    keys = jnp.dot(rows, key_matrix, preferred_element_type=jnp.float32)
    values = jnp.dot(rows, value_matrix, preferred_element_type=jnp.float32)
    half = keys.shape[1] // 2
    other = [(0, 1), (1, 0)]

    def pick(c):
        start = c * half
        return jnp.concatenate(
            [lax.dynamic_slice_in_dim(keys, start, half, 1), lax.dynamic_slice_in_dim(values, start, half, 1)], axis=1
        )

    mine = pick(core) + lax.ppermute(pick(1 - core), "seq", other)
    mine = mine.reshape(n_slots, 2, 2, HEAD_SIZE)
    kv = jnp.concatenate(
        [head_norm(mine[:, 0], key_gain).astype(jnp.bfloat16), mine[:, 1].astype(jnp.bfloat16)], axis=1
    ).reshape(n_slots, 4 * HEAD_SIZE)
    slots = image_slot.reshape(-1)
    one_hot = (slots[:, None] == jnp.arange(n_slots, dtype=jnp.int32)[None, :]).astype(jnp.bfloat16)
    packed = jnp.dot(one_hot, kv, preferred_element_type=jnp.float32).astype(jnp.bfloat16)
    packed = packed.reshape(image_slot.shape[0], IMG_MAX * 4 * HEAD_SIZE)
    got = lax.all_to_all(packed, "doc", split_axis=0, concat_axis=0, tiled=True)
    theirs = lax.ppermute(got, "seq", other)
    first = jnp.where(core == 0, got, theirs).reshape(-1, IMG_MAX, 2, 2, HEAD_SIZE)
    second = jnp.where(core == 0, theirs, got).reshape(-1, IMG_MAX, 2, 2, HEAD_SIZE)
    both = jnp.concatenate([first, second], axis=3)
    n_keys = both.shape[0] * IMG_MAX
    both = both.reshape(n_keys, 2, KEY_VALUE_HEADS, HEAD_SIZE)
    local_tokens = queries.shape[0]
    positions = core * local_tokens + jnp.arange(local_tokens, dtype=jnp.int32)
    q = queries.astype(jnp.float32).reshape(local_tokens, KEY_VALUE_HEADS, GROUP, HEAD_SIZE)
    q = head_norm(q, query_gain).astype(jnp.bfloat16)
    seen = jnp.arange(IMG_MAX, dtype=jnp.int32)
    attends = (
        (seen[None, :] < image_count[0])
        & (image_pos[0][None, :] <= positions[:, None])
        & (positions[:, None] < span_end[0][None, :])
    )
    scores = jnp.einsum("tkgd,nkd->tkgn", q, both[:, 0], preferred_element_type=jnp.float32)
    scores = scores * (1.0 / math.sqrt(HEAD_SIZE))
    key_mask = jnp.tile(attends, (1, n_keys // IMG_MAX))
    weights = jnp.where(key_mask[:, None, None, :], jnp.exp(scores), 0.0).astype(jnp.bfloat16)
    numerator = jnp.einsum("tkgn,nkd->tkgd", weights, both[:, 1], preferred_element_type=jnp.float32)
    denominator = jnp.sum(weights, axis=3, dtype=jnp.float32)
    reached = jnp.any(attends, axis=1)[:, None, None]
    quotient = numerator / jnp.where(reached, denominator, 1.0)[..., None]
    mixed_rows = jnp.where(reached[..., None], quotient, 0.0).astype(jnp.bfloat16)
    return mixed_rows.reshape(local_tokens, QUERY_HEADS * HEAD_SIZE)


def iota(shape, axis):
    return lax.broadcasted_iota(jnp.int32, shape, axis)


def flag(condition):
    return condition.astype(jnp.float32).astype(jnp.bfloat16)


def mm(a, b, contract=((1,), (0,))):
    return lax.dot_general(a, b, (contract, ((), ())), preferred_element_type=jnp.float32)


RIGHT = ((1,), (1,))


def fused_kernel(
    q_hbm,
    x_hbm,
    wk_hbm,
    wv_hbm,
    qg_ref,
    kg_ref,
    count_ref,
    slot_ref,
    pos_ref,
    end_ref,
    out_hbm,
    q_v,
    x_v,
    wk_v,
    wv_v,
    sum_k,
    sum_v,
    got_k,
    got_v,
    pick1,
    expand,
    send1,
    recv1,
    send2,
    recv2,
    q_send,
    q_all,
    q_tail,
    k_tail,
    o_sum,
    o_own,
    o_send,
    local_sem,
    w_sem,
    out_sem,
    part_sems,
    q_sems,
    o_sems,
    s1_sem,
    r1_sem,
    s2_sem,
    r2_sem,
):
    doc = lax.axis_index("doc")
    core = lax.axis_index("seq")
    sibling = 1 - core
    z, p = doc // PLANE, doc % PLANE
    px, py = p // 4, p % 4
    tokens = q_v.shape[0]
    n_slots, depth = x_v.shape
    piece = depth // PIECES
    row_block = n_slots // 4
    half = KEY_VALUE_HEADS // 2 * HEAD_SIZE
    own_half = pl.ds(pl.multiple_of(core * half, half), half)
    sib_half = pl.ds(pl.multiple_of(sibling * half, half), half)

    def x_copy(i):
        rows = pl.ds(i * row_block, row_block)
        return pltpu.make_async_copy(x_hbm.at[rows], x_v.at[rows], local_sem.at[i])

    q_copy = pltpu.make_async_copy(q_hbm, q_v, local_sem.at[4])

    def w_copy(i, c):
        rows = pl.ds(c * piece, piece)
        hbm, v = ((wk_hbm, wk_v), (wv_hbm, wv_v))[i]
        return pltpu.make_async_copy(hbm.at[rows], v.at[rows], w_sem.at[i, c])

    for i in range(4):
        x_copy(i).start()
    for c in range(PIECES):
        w_copy(0, c).start()
        w_copy(1, c).start()
    q_copy.start()

    def z_to(s):
        return (z + Z_STEPS[s]) % PLANES

    def plane_to(i):
        return ((px + i // 4) % 4) * 4 + (py + i % 4) % 4

    barrier = pltpu.get_barrier_semaphore()
    pl.semaphore_signal(barrier, inc=1, device_id=(doc, sibling), device_id_type=MESH)

    def greet_z(i, carry):
        there = ((z + i) % PLANES) * PLANE + p
        pl.semaphore_signal(barrier, inc=1, device_id=(there, core), device_id_type=MESH)
        return carry

    def greet_plane(i, carry):
        pl.semaphore_signal(barrier, inc=1, device_id=(z * PLANE + plane_to(i), core), device_id_type=MESH)
        return carry

    lax.fori_loop(1, PLANES, greet_z, 0)
    lax.fori_loop(1, PLANE, greet_plane, 0)

    slots_t = slot_ref[...]
    present = slots_t >= 0
    there = flag(present)
    d_row, d_col = iota((128, 128), 0), iota((128, 128), 1)
    same = (d_row // PLANE) == (d_col // PLANE)
    before = mm(there, flag(same & (d_row < d_col)))
    totals = mm(there, flag(same)).astype(jnp.bfloat16)
    earlier = mm(flag(iota((8, 8), 1) < iota((8, 8), 0)), totals)
    rank = before + earlier
    identity = flag(d_row == d_col)
    slot_cols = mm(identity, slots_t.astype(jnp.float32).astype(jnp.bfloat16), RIGHT)
    rank_cols = mm(identity, jnp.where(present, rank, 0.0).astype(jnp.bfloat16), RIGHT)
    away = (iota((128, 1), 0) // PLANE + PLANES - z) % PLANES
    z_slot = jnp.where(away == 0, 0, jnp.where(away <= PLANES // 2, 2 * away - 1, 2 * (PLANES - away)))
    plane_base = (CAPACITY * z_slot).astype(jnp.float32) + 1.0
    slot_lane = iota((1, n_slots), 1).astype(jnp.float32)
    found = jnp.zeros((128, n_slots), jnp.float32)
    for j in range(IMG_MAX):
        found = found + jnp.where(
            slot_cols[:, j : j + 1] == slot_lane, rank_cols[:, j : j + 1] + plane_base, 0.0
        )
    goes_to = jnp.sum(found, axis=0, keepdims=True) - 1.0
    pick1[...] = flag(iota((PLANES * CAPACITY, n_slots), 0).astype(jnp.float32) == goes_to)

    pair = 2 * IMG_MAX
    rows_e, cols_e = PLANE * pair, 2 * CAPACITY
    row_step = iota((rows_e, 128), 0) // pair
    row_doc = z * PLANE + ((px + row_step // 4) % 4) * 4 + (py + row_step % 4) % 4
    mine_doc = flag(iota((rows_e, 128), 1) == row_doc)
    rank_plus = jnp.where(present, rank + 1.0, 0.0).astype(jnp.bfloat16)
    by_slot = mm(mine_doc, rank_plus, RIGHT)
    chosen = iota((rows_e, IMG_MAX), 1) == iota((rows_e, IMG_MAX), 0) % IMG_MAX
    row_rank = jnp.sum(jnp.where(chosen, by_slot, 0.0), axis=1, keepdims=True)
    source = (iota((rows_e, 1), 0) // IMG_MAX) % 2
    row_target = jnp.where(row_rank > 0.0, row_rank - 1.0 + (CAPACITY * source).astype(jnp.float32), -1.0)
    expand[...] = flag(iota((rows_e, cols_e), 1).astype(jnp.float32) == row_target)

    lane = iota((1, HEAD_SIZE), 1)
    first_t = jnp.zeros((1, HEAD_SIZE), jnp.int32)
    last_t = jnp.zeros((1, HEAD_SIZE), jnp.int32)
    for j in range(IMG_MAX):
        first_t = jnp.where(lane == j, pos_ref[0, j], first_t)
        last_t = jnp.where(lane == j, end_ref[0, j], last_t)
    block = iota((2 * tokens, HEAD_SIZE), 0) // tokens
    owner = jnp.where(block == 0, core, sibling)
    t_pos = owner * tokens + iota((2 * tokens, HEAD_SIZE), 0) % tokens
    attends = (lane < count_ref[0]) & (first_t <= t_pos) & (t_pos < last_t)
    q_tail[...] = flag(jnp.logical_not(attends))
    n_keys = k_tail.shape[0]
    k_tail[...] = jnp.where(
        iota((n_keys, HEAD_SIZE), 1) == iota((n_keys, HEAD_SIZE), 0) % IMG_MAX, MASKED, 0.0
    ).astype(jnp.bfloat16)

    for i in range(4):
        x_copy(i).wait()
    for c in range(PIECES):
        cols = pl.ds(c * piece, piece)
        for i, (w, total) in enumerate(((wk_v, sum_k), (wv_v, sum_v))):
            w_copy(i, c).wait()
            term = mm(x_v[:, cols], w[cols, :])
            total[...] = term if c == 0 else total[...] + term

    def part_copy(i):
        total, got = ((sum_k, got_k), (sum_v, got_v))[i]
        return pltpu.make_async_remote_copy(
            src_ref=total.at[:, sib_half],
            dst_ref=got,
            send_sem=part_sems.at[0, i],
            recv_sem=part_sems.at[1, i],
            device_id=(doc, sibling),
            device_id_type=MESH,
        )

    pl.semaphore_wait(barrier, PLANES - 1 + PLANE - 1 + 1)
    part_copy(0).start()
    part_copy(1).start()

    q_copy.wait()
    q_gain = qg_ref[...]
    half_width = QUERY_HEADS // 2 * HEAD_SIZE

    def norm_queries(i, carry):
        at = pl.multiple_of(i * HEAD_SIZE, HEAD_SIZE)
        own_cols = pl.ds(pl.multiple_of(core * half_width + at, HEAD_SIZE), HEAD_SIZE)
        sib_cols = pl.ds(pl.multiple_of(sibling * half_width + at, HEAD_SIZE), HEAD_SIZE)
        q_all[0, :, pl.ds(at, HEAD_SIZE)] = head_norm(q_v[:, own_cols].astype(jnp.float32), q_gain).astype(jnp.bfloat16)
        q_send[:, pl.ds(at, HEAD_SIZE)] = head_norm(q_v[:, sib_cols].astype(jnp.float32), q_gain).astype(jnp.bfloat16)
        return carry

    def norm_all_queries():
        lax.fori_loop(0, QUERY_HEADS // 2, norm_queries, 0)

    q_exchange = pltpu.make_async_remote_copy(
        src_ref=q_send,
        dst_ref=q_all.at[1],
        send_sem=q_sems.at[0],
        recv_sem=q_sems.at[1],
        device_id=(doc, sibling),
        device_id_type=MESH,
    )

    def hop1(s):
        return pltpu.make_async_remote_copy(
            src_ref=send1.at[s],
            dst_ref=recv1.at[s],
            send_sem=s1_sem.at[s],
            recv_sem=r1_sem.at[s],
            device_id=(z_to(s) * PLANE + p, core),
            device_id_type=MESH,
        )

    def hop2(k, i):
        return pltpu.make_async_remote_copy(
            src_ref=send2.at[k, i],
            dst_ref=recv2.at[k, i],
            send_sem=s2_sem.at[k],
            recv_sem=r2_sem.at[k],
            device_id=(z * PLANE + plane_to(i), core),
            device_id_type=MESH,
        )

    def await_group(ref, k, sem):
        part = ref.at[k, pl.ds(1, PLANE - 1)]
        pltpu.make_async_copy(part, part, sem.at[k]).wait()

    key_gain = kg_ref[...]
    part_copy(0).wait_recv()
    raw_k = sum_k[:, own_half] + got_k[...]
    keys_own = [head_norm(raw_k[:, h * HEAD_SIZE : (h + 1) * HEAD_SIZE], key_gain).astype(jnp.bfloat16) for h in range(2)]
    part_copy(1).wait_recv()
    raw_v = (sum_v[:, own_half] + got_v[...]).astype(jnp.bfloat16)
    kv_own = jnp.concatenate(keys_own + [raw_v], axis=1)
    packed = mm(pick1[...], kv_own).astype(jnp.bfloat16).reshape(PLANES, CAPACITY, 2 * half)
    recv1[0] = packed[0]
    for s in range(1, PLANES):
        send1[s] = packed[s]
    for s in range(1, PLANES):
        hop1(s).start()
    norm_all_queries()
    q_exchange.start()

    def expand_and_send(k):
        for s in (2 * k, 2 * k + 1):
            if s > 0:
                hop1(s).wait_recv()
        rows = mm(expand[...], recv1[pl.ds(2 * k, 2)].reshape(2 * CAPACITY, 2 * half)).astype(jnp.bfloat16)
        rows = rows.reshape(PLANE, pair, 2 * half)
        recv2[k, 0] = rows[0]
        send2[k, pl.ds(1, PLANE - 1)] = rows[1:]

        def body(i, carry):
            hop2(k, i).start()
            return carry

        lax.fori_loop(1, PLANE, body, 0)

    ones = jnp.ones((n_keys, HEAD_SIZE), jnp.bfloat16)
    scale = 1.0 / math.sqrt(HEAD_SIZE)
    last = PLANES // 2 - 1

    def attend(k):
        await_group(recv2, k, r2_sem)

        def heads(n, carry):
            h = n // (GROUP // UNROLL)
            k_cols = pl.ds(pl.multiple_of(h * HEAD_SIZE, HEAD_SIZE), HEAD_SIZE)
            v_cols = pl.ds(pl.multiple_of(half + h * HEAD_SIZE, HEAD_SIZE), HEAD_SIZE)
            keys = jnp.concatenate([recv2[k, :, :, k_cols].reshape(n_keys, HEAD_SIZE), k_tail[...]], axis=1)
            values = jnp.concatenate([recv2[k, :, :, v_cols].reshape(n_keys, HEAD_SIZE), ones], axis=1)
            for u in range(UNROLL):
                g = n * UNROLL + u
                cols = pl.ds(pl.multiple_of(g * HEAD_SIZE, HEAD_SIZE), HEAD_SIZE)
                q = q_all[:, :, cols].reshape(2 * tokens, HEAD_SIZE)
                scores = mm(jnp.concatenate([q, q_tail[...]], axis=1), keys, RIGHT)
                weights = jnp.exp(scores * scale).astype(jnp.bfloat16)
                mixed = mm(weights, values)
                if k > 0:
                    mixed = mixed + o_sum[g]
                if k < last:
                    o_sum[g] = mixed
                else:
                    total = mixed[:, HEAD_SIZE:]
                    out = (mixed[:, :HEAD_SIZE] / jnp.where(total > 0.0, total, 1.0)).astype(jnp.bfloat16)
                    o_own[:, cols] = out[:tokens]
                    o_send[:, cols] = out[tokens:]
            return carry

        per_head = GROUP // UNROLL
        if k < last:
            lax.fori_loop(0, 2 * per_head, heads, 0)
        else:
            for h in range(2):
                lax.fori_loop(h * per_head, (h + 1) * per_head, heads, 0)
                o_copy(h).start()
                own_copy(h).start()

    out_width = GROUP * HEAD_SIZE

    def out_at(of, h):
        return out_hbm.at[:, pl.ds(pl.multiple_of((of * 2 + h) * out_width, out_width), out_width)]

    def o_copy(h):
        return pltpu.make_async_remote_copy(
            src_ref=o_send.at[:, pl.ds(h * out_width, out_width)],
            dst_ref=out_at(core, h),
            send_sem=o_sems.at[0, h],
            recv_sem=o_sems.at[1, h],
            device_id=(doc, sibling),
            device_id_type=MESH,
        )

    def o_in(h):
        return pltpu.make_async_remote_copy(
            src_ref=o_send.at[:, pl.ds(h * out_width, out_width)],
            dst_ref=out_at(sibling, h),
            send_sem=o_sems.at[0, h],
            recv_sem=o_sems.at[1, h],
            device_id=(doc, sibling),
            device_id_type=MESH,
        )

    def own_copy(h):
        return pltpu.make_async_copy(o_own.at[:, pl.ds(h * out_width, out_width)], out_at(core, h), out_sem.at[h])

    expand_and_send(0)
    expand_and_send(1)
    expand_and_send(2)
    q_exchange.wait_recv()
    attend(0)
    expand_and_send(3)
    attend(1)
    attend(2)
    attend(3)

    for i in range(2):
        part_copy(i).wait_send()
    for s in range(1, PLANES):
        hop1(s).wait_send()
    for k in range(last + 1):
        await_group(send2, k, s2_sem)
    q_exchange.wait_send()
    for h in range(2):
        o_copy(h).wait_send()
        own_copy(h).wait()
        o_in(h).wait_recv()


def packed_route(
    queries,
    vision,
    key_matrix,
    value_matrix,
    query_gain,
    key_gain,
    image_count,
    image_slot,
    image_pos,
    span_end,
):
    tokens, width = queries.shape
    n_slots = vision.shape[0]
    depth = vision.shape[2]
    two = 2 * HEAD_SIZE
    anywhere = pl.BlockSpec(memory_space=pl.ANY)
    vmem = pl.BlockSpec(memory_space=pltpu.VMEM)
    smem = pl.BlockSpec(memory_space=pltpu.SMEM)
    bf16, f32 = jnp.bfloat16, jnp.float32
    dma = pltpu.SemaphoreType.DMA
    groups = PLANES // 2
    pair = 2 * IMG_MAX
    out = pl.pallas_call(
        fused_kernel,
        out_shape=jax.ShapeDtypeStruct((tokens, width), bf16),
        in_specs=[anywhere, anywhere, anywhere, anywhere, vmem, vmem, smem, vmem, smem, smem],
        out_specs=anywhere,
        scratch_shapes=[
            pltpu.VMEM((tokens, width), bf16),
            pltpu.VMEM((n_slots, depth), bf16),
            pltpu.VMEM(key_matrix.shape, bf16),
            pltpu.VMEM(value_matrix.shape, bf16),
            pltpu.VMEM((n_slots, 2 * two), f32),
            pltpu.VMEM((n_slots, 2 * two), f32),
            pltpu.VMEM((n_slots, two), f32),
            pltpu.VMEM((n_slots, two), f32),
            pltpu.VMEM((PLANES * CAPACITY, n_slots), bf16),
            pltpu.VMEM((PLANE * pair, 2 * CAPACITY), bf16),
            pltpu.VMEM((PLANES, CAPACITY, 2 * two), bf16),
            pltpu.VMEM((PLANES, CAPACITY, 2 * two), bf16),
            pltpu.VMEM((groups, PLANE, pair, 2 * two), bf16),
            pltpu.VMEM((groups, PLANE, pair, 2 * two), bf16),
            pltpu.VMEM((tokens, width // 2), bf16),
            pltpu.VMEM((2, tokens, width // 2), bf16),
            pltpu.VMEM((2 * tokens, HEAD_SIZE), bf16),
            pltpu.VMEM((PLANE * pair, HEAD_SIZE), bf16),
            pltpu.VMEM((2 * GROUP, 2 * tokens, two), f32),
            pltpu.VMEM((tokens, width // 2), bf16),
            pltpu.VMEM((tokens, width // 2), bf16),
            dma((5,)),
            dma((2, PIECES)),
            dma((2,)),
            dma((2, 2)),
            dma((2,)),
            dma((2, 2)),
            dma((PLANES,)),
            dma((PLANES,)),
            dma((groups,)),
            dma((groups,)),
        ],
        compiler_params=pltpu.CompilerParams(
            collective_id=0, has_side_effects=True, vmem_limit_bytes=56 * 1024 * 1024
        ),
        name="fused_cross_attention",
    )(
        queries,
        vision.reshape(n_slots, depth),
        key_matrix,
        value_matrix,
        query_gain.reshape(1, HEAD_SIZE),
        key_gain.reshape(1, HEAD_SIZE),
        image_count,
        image_slot.T,
        image_pos,
        span_end,
    )
    return out


def shards(*arrays):
    image_slot = arrays[7]
    shift = 8 * (jnp.arange(image_slot.shape[0], dtype=jnp.uint32) // PLANE % 4)
    part = jnp.where(image_slot >= 0, jnp.uint32(1) << shift[:, None], jnp.uint32(0))
    words = [jnp.sum(part[: 4 * PLANE]), jnp.sum(part[4 * PLANE :])]
    fits = jnp.bool_(True)
    for word in words:
        for i in range(4):
            fits = fits & (((word >> (8 * i)) & 255) <= CAPACITY)
    return lax.cond(fits, packed_route, general_route, *arrays)

def solution(mesh):
    in_specs = (
        P(("doc", "seq"), None),
        P(None, "doc", "seq"),
        P("seq", None),
        P("seq", None),
        P(),
        P(),
        P("doc"),
        P(),
        P("doc", None),
        P("doc", None),
    )
    out_specs = P(("doc", "seq"), None)
    return jax.shard_map(shards, mesh=mesh, in_specs=in_specs, out_specs=out_specs, check_vma=False)
```

```python
import functools
import math

import jax
import jax.numpy as jnp
from jax import lax
from jax.experimental import pallas as pl
from jax.experimental.pallas import tpu as pltpu
from jax.sharding import PartitionSpec as P

HEAD_SIZE = 128
QUERY_HEADS = 32
KEY_VALUE_HEADS = 4
IMG_MAX = 8
GROUP = QUERY_HEADS // KEY_VALUE_HEADS
PLANE = 16
PLANES = 8
CAPACITY = 48
MESH = pl.DeviceIdType.MESH
MASKED = -32768.0
PIECES = 8
AHEAD = 3
Z_STEPS = (0, 1, 7, 2, 6, 3, 5, 4)

epsilon = 1e-05


def head_norm(values, scales):
    mean_square = jnp.mean(values * values, axis=-1, keepdims=True)
    return values * lax.rsqrt(mean_square + epsilon) * scales


def general_route(
    queries,
    vision,
    key_matrix,
    value_matrix,
    query_gain,
    key_gain,
    image_count,
    image_slot,
    image_pos,
    span_end,
):
    n_slots = vision.shape[0]
    core = lax.axis_index("seq")
    rows = vision.reshape(n_slots, -1)
    keys = jnp.dot(rows, key_matrix, preferred_element_type=jnp.float32)
    values = jnp.dot(rows, value_matrix, preferred_element_type=jnp.float32)
    half = keys.shape[1] // 2
    other = [(0, 1), (1, 0)]

    def pick(c):
        start = c * half
        return jnp.concatenate(
            [lax.dynamic_slice_in_dim(keys, start, half, 1), lax.dynamic_slice_in_dim(values, start, half, 1)], axis=1
        )

    mine = pick(core) + lax.ppermute(pick(1 - core), "seq", other)
    mine = mine.reshape(n_slots, 2, 2, HEAD_SIZE)
    kv = jnp.concatenate(
        [head_norm(mine[:, 0], key_gain).astype(jnp.bfloat16), mine[:, 1].astype(jnp.bfloat16)], axis=1
    ).reshape(n_slots, 4 * HEAD_SIZE)
    slots = image_slot.reshape(-1)
    one_hot = (slots[:, None] == jnp.arange(n_slots, dtype=jnp.int32)[None, :]).astype(jnp.bfloat16)
    packed = jnp.dot(one_hot, kv, preferred_element_type=jnp.float32).astype(jnp.bfloat16)
    packed = packed.reshape(image_slot.shape[0], IMG_MAX * 4 * HEAD_SIZE)
    got = lax.all_to_all(packed, "doc", split_axis=0, concat_axis=0, tiled=True)
    theirs = lax.ppermute(got, "seq", other)
    first = jnp.where(core == 0, got, theirs).reshape(-1, IMG_MAX, 2, 2, HEAD_SIZE)
    second = jnp.where(core == 0, theirs, got).reshape(-1, IMG_MAX, 2, 2, HEAD_SIZE)
    both = jnp.concatenate([first, second], axis=3)
    n_keys = both.shape[0] * IMG_MAX
    both = both.reshape(n_keys, 2, KEY_VALUE_HEADS, HEAD_SIZE)
    local_tokens = queries.shape[0]
    positions = core * local_tokens + jnp.arange(local_tokens, dtype=jnp.int32)
    q = queries.astype(jnp.float32).reshape(local_tokens, KEY_VALUE_HEADS, GROUP, HEAD_SIZE)
    q = head_norm(q, query_gain).astype(jnp.bfloat16)
    seen = jnp.arange(IMG_MAX, dtype=jnp.int32)
    attends = (
        (seen[None, :] < image_count[0])
        & (image_pos[0][None, :] <= positions[:, None])
        & (positions[:, None] < span_end[0][None, :])
    )
    scores = jnp.einsum("tkgd,nkd->tkgn", q, both[:, 0], preferred_element_type=jnp.float32)
    scores = scores * (1.0 / math.sqrt(HEAD_SIZE))
    key_mask = jnp.tile(attends, (1, n_keys // IMG_MAX))
    weights = jnp.where(key_mask[:, None, None, :], jnp.exp(scores), 0.0).astype(jnp.bfloat16)
    numerator = jnp.einsum("tkgn,nkd->tkgd", weights, both[:, 1], preferred_element_type=jnp.float32)
    denominator = jnp.sum(weights, axis=3, dtype=jnp.float32)
    reached = jnp.any(attends, axis=1)[:, None, None]
    quotient = numerator / jnp.where(reached, denominator, 1.0)[..., None]
    mixed_rows = jnp.where(reached[..., None], quotient, 0.0).astype(jnp.bfloat16)
    return mixed_rows.reshape(local_tokens, QUERY_HEADS * HEAD_SIZE)


def iota(shape, axis):
    return lax.broadcasted_iota(jnp.int32, shape, axis)


def flag(condition):
    return condition.astype(jnp.float32).astype(jnp.bfloat16)


def mm(a, b, contract=((1,), (0,))):
    return lax.dot_general(a, b, (contract, ((), ())), preferred_element_type=jnp.float32)


RIGHT = ((1,), (1,))


def fused_kernel(
    q_hbm,
    x_hbm,
    wk_hbm,
    wv_hbm,
    qg_ref,
    kg_ref,
    count_ref,
    slot_ref,
    pos_ref,
    end_ref,
    out_hbm,
    q_v,
    x_v,
    wk_v,
    wv_v,
    sum_k,
    sum_v,
    got_k,
    got_v,
    pick1,
    expand,
    send1,
    recv1,
    send2,
    recv2,
    q_send,
    q_own,
    q_sib,
    q_tail,
    k_tail,
    o_sum,
    o_own,
    o_send,
    local_sem,
    w_sem,
    out_sem,
    part_sems,
    q_sems,
    o_sems,
    s1_sem,
    r1_sem,
    s2_sem,
    r2_sem,
):
    doc = lax.axis_index("doc")
    core = lax.axis_index("seq")
    sibling = 1 - core
    z, p = doc // PLANE, doc % PLANE
    px, py = p // 4, p % 4
    tokens, width = q_v.shape
    n_slots, depth = x_v.shape
    piece = depth // PIECES
    row_block = n_slots // 4
    half = KEY_VALUE_HEADS // 2 * HEAD_SIZE
    own_half = pl.ds(pl.multiple_of(core * half, half), half)
    sib_half = pl.ds(pl.multiple_of(sibling * half, half), half)

    def x_copy(i):
        rows = pl.ds(i * row_block, row_block)
        return pltpu.make_async_copy(x_hbm.at[rows], x_v.at[rows], local_sem.at[i])

    q_copy = pltpu.make_async_copy(q_hbm, q_v, local_sem.at[4])

    def w_copy(i, c):
        rows = pl.ds(c * piece, piece)
        hbm, v = ((wk_hbm, wk_v), (wv_hbm, wv_v))[i]
        return pltpu.make_async_copy(hbm.at[rows], v.at[rows], w_sem.at[i, c])

    for i in range(4):
        x_copy(i).start()
    for c in range(AHEAD):
        w_copy(0, c).start()
        w_copy(1, c).start()

    def z_to(s):
        return (z + Z_STEPS[s]) % PLANES

    def plane_to(i):
        return ((px + i // 4) % 4) * 4 + (py + i % 4) % 4

    barrier = pltpu.get_barrier_semaphore()
    pl.semaphore_signal(barrier, inc=1, device_id=(doc, sibling), device_id_type=MESH)

    def greet_z(i, carry):
        there = ((z + i) % PLANES) * PLANE + p
        pl.semaphore_signal(barrier, inc=1, device_id=(there, core), device_id_type=MESH)
        return carry

    def greet_plane(i, carry):
        pl.semaphore_signal(barrier, inc=1, device_id=(z * PLANE + plane_to(i), core), device_id_type=MESH)
        return carry

    lax.fori_loop(1, PLANES, greet_z, 0)
    lax.fori_loop(1, PLANE, greet_plane, 0)

    slots_t = slot_ref[...]
    present = slots_t >= 0
    there = flag(present)
    d_row, d_col = iota((128, 128), 0), iota((128, 128), 1)
    same = (d_row // PLANE) == (d_col // PLANE)
    before = mm(there, flag(same & (d_row < d_col)))
    totals = mm(there, flag(same)).astype(jnp.bfloat16)
    earlier = mm(flag(iota((8, 8), 1) < iota((8, 8), 0)), totals)
    rank = before + earlier
    identity = flag(d_row == d_col)
    slot_cols = mm(identity, slots_t.astype(jnp.float32).astype(jnp.bfloat16), RIGHT)
    rank_cols = mm(identity, jnp.where(present, rank, 0.0).astype(jnp.bfloat16), RIGHT)
    away = (iota((128, 1), 0) // PLANE + PLANES - z) % PLANES
    z_slot = jnp.where(away == 0, 0, jnp.where(away <= PLANES // 2, 2 * away - 1, 2 * (PLANES - away)))
    plane_base = (CAPACITY * z_slot).astype(jnp.float32) + 1.0
    slot_lane = iota((1, n_slots), 1).astype(jnp.float32)
    found = jnp.zeros((128, n_slots), jnp.float32)
    for j in range(IMG_MAX):
        found = found + jnp.where(
            slot_cols[:, j : j + 1] == slot_lane, rank_cols[:, j : j + 1] + plane_base, 0.0
        )
    goes_to = jnp.sum(found, axis=0, keepdims=True) - 1.0
    pick1[...] = flag(iota((PLANES * CAPACITY, n_slots), 0).astype(jnp.float32) == goes_to)

    lane = iota((1, HEAD_SIZE), 1)
    first_t = jnp.zeros((1, HEAD_SIZE), jnp.int32)
    last_t = jnp.zeros((1, HEAD_SIZE), jnp.int32)
    for j in range(IMG_MAX):
        first_t = jnp.where(lane == j, pos_ref[0, j], first_t)
        last_t = jnp.where(lane == j, end_ref[0, j], last_t)
    block = iota((4 * tokens, HEAD_SIZE), 0) // (2 * tokens)
    owner = jnp.where(block == 0, core, sibling)
    t_pos = owner * tokens + iota((4 * tokens, HEAD_SIZE), 0) % tokens
    attends = (lane < count_ref[0]) & (first_t <= t_pos) & (t_pos < last_t)
    q_tail[...] = flag(jnp.logical_not(attends))
    n_keys = k_tail.shape[0]
    k_tail[...] = jnp.where(
        iota((n_keys, HEAD_SIZE), 1) == iota((n_keys, HEAD_SIZE), 0) % IMG_MAX, MASKED, 0.0
    ).astype(jnp.bfloat16)

    for i in range(4):
        x_copy(i).wait()
    for c in range(PIECES):
        cols = pl.ds(c * piece, piece)
        for i, (w, total) in enumerate(((wk_v, sum_k), (wv_v, sum_v))):
            w_copy(i, c).wait()
            if c + AHEAD < PIECES:
                w_copy(i, c + AHEAD).start()
            elif c + AHEAD == PIECES and i == 0:
                q_copy.start()
            term = mm(x_v[:, cols], w[cols, :])
            total[...] = term if c == 0 else total[...] + term

    def part_copy(i):
        total, got = ((sum_k, got_k), (sum_v, got_v))[i]
        return pltpu.make_async_remote_copy(
            src_ref=total.at[:, sib_half],
            dst_ref=got,
            send_sem=part_sems.at[0, i],
            recv_sem=part_sems.at[1, i],
            device_id=(doc, sibling),
            device_id_type=MESH,
        )

    pl.semaphore_wait(barrier, PLANES - 1 + PLANE - 1 + 1)
    part_copy(0).start()
    part_copy(1).start()

    q_copy.wait()
    q_gain = qg_ref[...]
    half_width = QUERY_HEADS // 2 * HEAD_SIZE

    def norm_queries(n, carry):
        for u in range(4):
            i = n * 4 + u
            at = pl.multiple_of(i * HEAD_SIZE, HEAD_SIZE)
            own_cols = pl.ds(pl.multiple_of(core * half_width + at, HEAD_SIZE), HEAD_SIZE)
            sib_cols = pl.ds(pl.multiple_of(sibling * half_width + at, HEAD_SIZE), HEAD_SIZE)
            q_own[i] = head_norm(q_v[:, own_cols].astype(jnp.float32), q_gain).astype(jnp.bfloat16)
            q_send[i] = head_norm(q_v[:, sib_cols].astype(jnp.float32), q_gain).astype(jnp.bfloat16)
        return carry

    lax.fori_loop(0, QUERY_HEADS // 8, norm_queries, 0)
    q_exchange = pltpu.make_async_remote_copy(
        src_ref=q_send,
        dst_ref=q_sib,
        send_sem=q_sems.at[0],
        recv_sem=q_sems.at[1],
        device_id=(doc, sibling),
        device_id_type=MESH,
    )

    q_exchange.start()

    def hop1(s):
        return pltpu.make_async_remote_copy(
            src_ref=send1.at[s],
            dst_ref=recv1.at[s],
            send_sem=s1_sem.at[s],
            recv_sem=r1_sem.at[s],
            device_id=(z_to(s) * PLANE + p, core),
            device_id_type=MESH,
        )

    def hop2(k, i):
        return pltpu.make_async_remote_copy(
            src_ref=send2.at[k, i],
            dst_ref=recv2.at[k, i],
            send_sem=s2_sem.at[k],
            recv_sem=r2_sem.at[k],
            device_id=(z * PLANE + plane_to(i), core),
            device_id_type=MESH,
        )

    def await_group(ref, k, sem):
        part = ref.at[k, pl.ds(1, PLANE - 1)]
        pltpu.make_async_copy(part, part, sem.at[k]).wait()

    key_gain = kg_ref[...]
    part_copy(0).wait_recv()
    raw_k = sum_k[:, own_half] + got_k[...]
    keys_own = [head_norm(raw_k[:, h * HEAD_SIZE : (h + 1) * HEAD_SIZE], key_gain).astype(jnp.bfloat16) for h in range(2)]
    part_copy(1).wait_recv()
    raw_v = (sum_v[:, own_half] + got_v[...]).astype(jnp.bfloat16)
    kv_own = jnp.concatenate(keys_own + [raw_v], axis=1)
    packed = mm(pick1[...], kv_own).astype(jnp.bfloat16).reshape(PLANES, CAPACITY, 2 * half)
    recv1[0] = packed[0]
    for s in range(1, PLANES):
        send1[s] = packed[s]
    for s in range(1, PLANES):
        hop1(s).start()
    pair = 2 * IMG_MAX
    rows_e, cols_e = PLANE * pair, 2 * CAPACITY
    row_step = iota((rows_e, 128), 0) // pair
    row_doc = z * PLANE + ((px + row_step // 4) % 4) * 4 + (py + row_step % 4) % 4
    mine_doc = flag(iota((rows_e, 128), 1) == row_doc)
    rank_plus = jnp.where(present, rank + 1.0, 0.0).astype(jnp.bfloat16)
    by_slot = mm(mine_doc, rank_plus, RIGHT)
    chosen = iota((rows_e, IMG_MAX), 1) == iota((rows_e, IMG_MAX), 0) % IMG_MAX
    row_rank = jnp.sum(jnp.where(chosen, by_slot, 0.0), axis=1, keepdims=True)
    source = (iota((rows_e, 1), 0) // IMG_MAX) % 2
    row_target = jnp.where(row_rank > 0.0, row_rank - 1.0 + (CAPACITY * source).astype(jnp.float32), -1.0)
    expand[...] = flag(iota((rows_e, cols_e), 1).astype(jnp.float32) == row_target)

    def expand_and_send(k):
        for s in (2 * k, 2 * k + 1):
            if s > 0:
                hop1(s).wait_recv()
        rows = mm(expand[...], recv1[pl.ds(2 * k, 2)].reshape(2 * CAPACITY, 2 * half)).astype(jnp.bfloat16)
        rows = rows.reshape(PLANE, pair, 2 * half)
        recv2[k, 0] = rows[0]
        send2[k, pl.ds(1, PLANE - 1)] = rows[1:]

        def body(i, carry):
            hop2(k, i).start()
            return carry

        lax.fori_loop(1, PLANE, body, 0)

    ones = jnp.ones((n_keys, HEAD_SIZE), jnp.bfloat16)
    scale = 1.0 / math.sqrt(HEAD_SIZE)
    last = PLANES // 2 - 1

    blocks = GROUP
    per_head = blocks // 2

    def attend(k):
        await_group(recv2, k, r2_sem)

        def keys_of(b):
            at = (b // per_head) * HEAD_SIZE
            rows = recv2[k, :, :, at : at + HEAD_SIZE].reshape(n_keys, HEAD_SIZE)
            return jnp.concatenate([rows, k_tail[...]], axis=1)

        def values_of(b):
            at = half + (b // per_head) * HEAD_SIZE
            rows = recv2[k, :, :, at : at + HEAD_SIZE].reshape(n_keys, HEAD_SIZE)
            return jnp.concatenate([rows, ones], axis=1)

        def scores_of(b):
            own = q_own[2 * b : 2 * b + 2].reshape(2 * tokens, HEAD_SIZE)
            sib = q_sib[2 * b : 2 * b + 2].reshape(2 * tokens, HEAD_SIZE)
            rows = jnp.concatenate([jnp.concatenate([own, sib], axis=0), q_tail[...]], axis=1)
            return mm(rows, keys_of(b), RIGHT)

        scores = scores_of(0)
        for b in range(blocks):
            weights = jnp.exp(scores * scale).astype(jnp.bfloat16)
            if b + 1 < blocks:
                scores = scores_of(b + 1)
            mixed = mm(weights, values_of(b))
            if k > 0:
                mixed = mixed + o_sum[b]
            if k < last:
                o_sum[b] = mixed
                continue
            total = mixed[:, HEAD_SIZE:]
            out = (mixed[:, :HEAD_SIZE] / jnp.where(total > 0.0, total, 1.0)).astype(jnp.bfloat16)
            for i in range(2):
                at = (2 * b + i) * HEAD_SIZE
                o_own[:, at : at + HEAD_SIZE] = out[i * tokens : (i + 1) * tokens]
                o_send[:, at : at + HEAD_SIZE] = out[(2 + i) * tokens : (3 + i) * tokens]
            if b % 2 == 1:
                o_copy(b // 2).start()
                own_copy(b // 2).start()

    quarters = 4
    out_width = width // 2 // quarters

    def out_at(of, h):
        return out_hbm.at[:, pl.ds(pl.multiple_of((of * quarters + h) * out_width, out_width), out_width)]

    def o_copy(h):
        return pltpu.make_async_remote_copy(
            src_ref=o_send.at[:, pl.ds(h * out_width, out_width)],
            dst_ref=out_at(core, h),
            send_sem=o_sems.at[0, h],
            recv_sem=o_sems.at[1, h],
            device_id=(doc, sibling),
            device_id_type=MESH,
        )

    def o_in(h):
        return pltpu.make_async_remote_copy(
            src_ref=o_send.at[:, pl.ds(h * out_width, out_width)],
            dst_ref=out_at(sibling, h),
            send_sem=o_sems.at[0, h],
            recv_sem=o_sems.at[1, h],
            device_id=(doc, sibling),
            device_id_type=MESH,
        )

    def own_copy(h):
        return pltpu.make_async_copy(o_own.at[:, pl.ds(h * out_width, out_width)], out_at(core, h), out_sem.at[h])

    expand_and_send(0)
    expand_and_send(1)
    expand_and_send(2)
    q_exchange.wait_recv()
    attend(0)
    expand_and_send(3)
    attend(1)
    attend(2)
    attend(3)

    for i in range(2):
        part_copy(i).wait_send()
    for s in range(1, PLANES):
        hop1(s).wait_send()
    for k in range(last + 1):
        await_group(send2, k, s2_sem)
    q_exchange.wait_send()
    for h in range(quarters):
        o_copy(h).wait_send()
        own_copy(h).wait()
        o_in(h).wait_recv()


def packed_route(
    queries,
    vision,
    key_matrix,
    value_matrix,
    query_gain,
    key_gain,
    image_count,
    image_slot,
    image_pos,
    span_end,
):
    tokens, width = queries.shape
    n_slots = vision.shape[0]
    depth = vision.shape[2]
    two = 2 * HEAD_SIZE
    anywhere = pl.BlockSpec(memory_space=pl.ANY)
    vmem = pl.BlockSpec(memory_space=pltpu.VMEM)
    smem = pl.BlockSpec(memory_space=pltpu.SMEM)
    bf16, f32 = jnp.bfloat16, jnp.float32
    dma = pltpu.SemaphoreType.DMA
    groups = PLANES // 2
    pair = 2 * IMG_MAX
    out = pl.pallas_call(
        fused_kernel,
        out_shape=jax.ShapeDtypeStruct((tokens, width), bf16),
        in_specs=[anywhere, anywhere, anywhere, anywhere, vmem, vmem, smem, vmem, smem, smem],
        out_specs=anywhere,
        scratch_shapes=[
            pltpu.VMEM((tokens, width), bf16),
            pltpu.VMEM((n_slots, depth), bf16),
            pltpu.VMEM(key_matrix.shape, bf16),
            pltpu.VMEM(value_matrix.shape, bf16),
            pltpu.VMEM((n_slots, 2 * two), f32),
            pltpu.VMEM((n_slots, 2 * two), f32),
            pltpu.VMEM((n_slots, two), f32),
            pltpu.VMEM((n_slots, two), f32),
            pltpu.VMEM((PLANES * CAPACITY, n_slots), bf16),
            pltpu.VMEM((PLANE * pair, 2 * CAPACITY), bf16),
            pltpu.VMEM((PLANES, CAPACITY, 2 * two), bf16),
            pltpu.VMEM((PLANES, CAPACITY, 2 * two), bf16),
            pltpu.VMEM((groups, PLANE, pair, 2 * two), bf16),
            pltpu.VMEM((groups, PLANE, pair, 2 * two), bf16),
            pltpu.VMEM((QUERY_HEADS // 2, tokens, HEAD_SIZE), bf16),
            pltpu.VMEM((QUERY_HEADS // 2, tokens, HEAD_SIZE), bf16),
            pltpu.VMEM((QUERY_HEADS // 2, tokens, HEAD_SIZE), bf16),
            pltpu.VMEM((4 * tokens, HEAD_SIZE), bf16),
            pltpu.VMEM((PLANE * pair, HEAD_SIZE), bf16),
            pltpu.VMEM((GROUP, 4 * tokens, two), f32),
            pltpu.VMEM((tokens, width // 2), bf16),
            pltpu.VMEM((tokens, width // 2), bf16),
            dma((5,)),
            dma((2, PIECES)),
            dma((4,)),
            dma((2, 2)),
            dma((2,)),
            dma((2, 4)),
            dma((PLANES,)),
            dma((PLANES,)),
            dma((groups,)),
            dma((groups,)),
        ],
        compiler_params=pltpu.CompilerParams(
            collective_id=0, has_side_effects=True, vmem_limit_bytes=56 * 1024 * 1024
        ),
        name="fused_cross_attention",
    )(
        queries,
        vision.reshape(n_slots, depth),
        key_matrix,
        value_matrix,
        query_gain.reshape(1, HEAD_SIZE),
        key_gain.reshape(1, HEAD_SIZE),
        image_count,
        image_slot.T,
        image_pos,
        span_end,
    )
    return out


def fits_kernel(slot_ref, fits_ref):
    same = (iota((128, 128), 0) // PLANE) == (iota((128, 128), 1) // PLANE)
    totals = mm(flag(slot_ref[...] >= 0), flag(same))
    crowded = jnp.max(jnp.sum(totals, axis=0, keepdims=True))
    fits_ref[0] = jnp.where(crowded <= CAPACITY, 1, 0)


def shards(*arrays):
    image_slot = arrays[7]
    fits = pl.pallas_call(
        fits_kernel,
        out_shape=jax.ShapeDtypeStruct((1,), jnp.int32),
        in_specs=[pl.BlockSpec(memory_space=pltpu.VMEM)],
        out_specs=pl.BlockSpec(memory_space=pltpu.SMEM),
        name="fits",
    )(image_slot.T)
    return lax.cond(fits[0] > 0, packed_route, general_route, *arrays)

def solution(mesh):
    in_specs = (
        P(("doc", "seq"), None),
        P(None, "doc", "seq"),
        P("seq", None),
        P("seq", None),
        P(),
        P(),
        P("doc"),
        P(),
        P("doc", None),
        P("doc", None),
    )
    out_specs = P(("doc", "seq"), None)
    return jax.shard_map(shards, mesh=mesh, in_specs=in_specs, out_specs=out_specs, check_vma=False)
```

```python
import functools
import math

import jax
import jax.numpy as jnp
from jax import lax
from jax.experimental import pallas as pl
from jax.experimental.pallas import tpu as pltpu
from jax.sharding import PartitionSpec as P

HEAD_SIZE = 128
QUERY_HEADS = 32
KEY_VALUE_HEADS = 4
IMG_MAX = 8
GROUP = QUERY_HEADS // KEY_VALUE_HEADS
PLANE = 16
PLANES = 8
CAPACITY = 48
SIDE = 4
GROUP_CAPACITY = 16
MESH = pl.DeviceIdType.MESH
MASKED = -32768.0
PIECES = 8
AHEAD = 3
Z_ORDER = (0, 1, 7, 2, 6, 3, 5, 4)

epsilon = 1e-05


def head_norm(values, scales):
    mean_square = jnp.mean(values * values, axis=-1, keepdims=True)
    return values * lax.rsqrt(mean_square + epsilon) * scales


def general_route(
    queries,
    vision,
    key_matrix,
    value_matrix,
    query_gain,
    key_gain,
    image_count,
    image_slot,
    image_pos,
    span_end,
):
    n_slots = vision.shape[0]
    core = lax.axis_index("seq")
    rows = vision.reshape(n_slots, -1)
    keys = jnp.dot(rows, key_matrix, preferred_element_type=jnp.float32)
    values = jnp.dot(rows, value_matrix, preferred_element_type=jnp.float32)
    half = keys.shape[1] // 2
    other = [(0, 1), (1, 0)]

    def pick(c):
        start = c * half
        return jnp.concatenate(
            [lax.dynamic_slice_in_dim(keys, start, half, 1), lax.dynamic_slice_in_dim(values, start, half, 1)], axis=1
        )

    mine = pick(core) + lax.ppermute(pick(1 - core), "seq", other)
    mine = mine.reshape(n_slots, 2, 2, HEAD_SIZE)
    kv = jnp.concatenate(
        [head_norm(mine[:, 0], key_gain).astype(jnp.bfloat16), mine[:, 1].astype(jnp.bfloat16)], axis=1
    ).reshape(n_slots, 4 * HEAD_SIZE)
    slots = image_slot.reshape(-1)
    one_hot = (slots[:, None] == jnp.arange(n_slots, dtype=jnp.int32)[None, :]).astype(jnp.bfloat16)
    packed = jnp.dot(one_hot, kv, preferred_element_type=jnp.float32).astype(jnp.bfloat16)
    packed = packed.reshape(image_slot.shape[0], IMG_MAX * 4 * HEAD_SIZE)
    got = lax.all_to_all(packed, "doc", split_axis=0, concat_axis=0, tiled=True)
    theirs = lax.ppermute(got, "seq", other)
    first = jnp.where(core == 0, got, theirs).reshape(-1, IMG_MAX, 2, 2, HEAD_SIZE)
    second = jnp.where(core == 0, theirs, got).reshape(-1, IMG_MAX, 2, 2, HEAD_SIZE)
    both = jnp.concatenate([first, second], axis=3)
    n_keys = both.shape[0] * IMG_MAX
    both = both.reshape(n_keys, 2, KEY_VALUE_HEADS, HEAD_SIZE)
    local_tokens = queries.shape[0]
    positions = core * local_tokens + jnp.arange(local_tokens, dtype=jnp.int32)
    q = queries.astype(jnp.float32).reshape(local_tokens, KEY_VALUE_HEADS, GROUP, HEAD_SIZE)
    q = head_norm(q, query_gain).astype(jnp.bfloat16)
    seen = jnp.arange(IMG_MAX, dtype=jnp.int32)
    attends = (
        (seen[None, :] < image_count[0])
        & (image_pos[0][None, :] <= positions[:, None])
        & (positions[:, None] < span_end[0][None, :])
    )
    scores = jnp.einsum("tkgd,nkd->tkgn", q, both[:, 0], preferred_element_type=jnp.float32)
    scores = scores * (1.0 / math.sqrt(HEAD_SIZE))
    key_mask = jnp.tile(attends, (1, n_keys // IMG_MAX))
    weights = jnp.where(key_mask[:, None, None, :], jnp.exp(scores), 0.0).astype(jnp.bfloat16)
    numerator = jnp.einsum("tkgn,nkd->tkgd", weights, both[:, 1], preferred_element_type=jnp.float32)
    denominator = jnp.sum(weights, axis=3, dtype=jnp.float32)
    reached = jnp.any(attends, axis=1)[:, None, None]
    quotient = numerator / jnp.where(reached, denominator, 1.0)[..., None]
    mixed_rows = jnp.where(reached[..., None], quotient, 0.0).astype(jnp.bfloat16)
    return mixed_rows.reshape(local_tokens, QUERY_HEADS * HEAD_SIZE)


def iota(shape, axis):
    return lax.broadcasted_iota(jnp.int32, shape, axis)


def flag(condition):
    return condition.astype(jnp.float32).astype(jnp.bfloat16)


def mm(a, b, contract=((1,), (0,))):
    return lax.dot_general(a, b, (contract, ((), ())), preferred_element_type=jnp.float32)


RIGHT = ((1,), (1,))


def z_slot_of(plane):
    return jnp.where(plane == 0, 0, jnp.where(plane <= PLANES // 2, 2 * plane - 1, 2 * (PLANES - plane)))


def fused_kernel(
    q_hbm,
    x_hbm,
    wk_hbm,
    wv_hbm,
    qg_ref,
    kg_ref,
    count_ref,
    slot_ref,
    pos_ref,
    end_ref,
    out_hbm,
    q_v,
    x_v,
    wk_v,
    wv_v,
    sum_k,
    sum_v,
    got_k,
    got_v,
    pick1,
    pick2,
    expand,
    send1,
    recv1,
    send_a,
    recv_a,
    send2,
    recv2,
    q_send,
    q_own,
    q_sib,
    q_tail,
    k_tail,
    o_sum,
    o_own,
    o_send,
    local_sem,
    w_sem,
    out_sem,
    part_sems,
    q_sems,
    o_sems,
    s1_sem,
    r1_sem,
    sa_sem,
    ra_sem,
    s2_sem,
    r2_sem,
):
    doc = lax.axis_index("doc")
    core = lax.axis_index("seq")
    sibling = 1 - core
    z, p = doc // PLANE, doc % PLANE
    px, py = p // SIDE, p % SIDE
    a = jnp.where(core == 0, px, py)
    b = jnp.where(core == 0, py, px)
    step_a = 1 + (SIDE - 1) * (1 - core)
    step_b = 1 + (SIDE - 1) * core
    tokens, width = q_v.shape
    n_slots, depth = x_v.shape
    piece = depth // PIECES
    row_block = n_slots // 4
    half = KEY_VALUE_HEADS // 2 * HEAD_SIZE
    own_half = pl.ds(pl.multiple_of(core * half, half), half)
    sib_half = pl.ds(pl.multiple_of(sibling * half, half), half)

    def x_copy(i):
        rows = pl.ds(i * row_block, row_block)
        return pltpu.make_async_copy(x_hbm.at[rows], x_v.at[rows], local_sem.at[i])

    q_copy = pltpu.make_async_copy(q_hbm, q_v, local_sem.at[4])

    def w_copy(i, c):
        rows = pl.ds(c * piece, piece)
        hbm, v = ((wk_hbm, wk_v), (wv_hbm, wv_v))[i]
        return pltpu.make_async_copy(hbm.at[rows], v.at[rows], w_sem.at[i, c])

    for i in range(4):
        x_copy(i).start()
    for c in range(AHEAD):
        w_copy(0, c).start()
        w_copy(1, c).start()

    own_slot = z_slot_of(z)

    def along_a(i):
        return (a + i) % SIDE * step_a + b * step_b

    def along_b(i):
        return a * step_a + (b + i) % SIDE * step_b

    barrier = pltpu.get_barrier_semaphore()
    pl.semaphore_signal(barrier, inc=1, device_id=(doc, sibling), device_id_type=MESH)

    def greet_z(i, carry):
        there = ((z + i) % PLANES) * PLANE + p
        pl.semaphore_signal(barrier, inc=1, device_id=(there, core), device_id_type=MESH)
        return carry

    lax.fori_loop(1, PLANES, greet_z, 0)
    for i in range(1, SIDE):
        for near in (along_a(i), along_b(i)):
            pl.semaphore_signal(barrier, inc=1, device_id=(z * PLANE + near, core), device_id_type=MESH)

    slots_t = slot_ref[...]
    present = slots_t >= 0
    there = flag(present)
    d_row, d_col = iota((128, 128), 0), iota((128, 128), 1)
    same = (d_row // PLANE) == (d_col // PLANE)
    first_order = flag(iota((8, 8), 1) < iota((8, 8), 0))

    def rank_within(same):
        before = mm(there, flag(same & (d_row < d_col)))
        totals = mm(there, flag(same)).astype(jnp.bfloat16)
        return before + mm(first_order, totals)

    rank = rank_within(same)
    identity = flag(d_row == d_col)
    slot_cols = mm(identity, slots_t.astype(jnp.float32).astype(jnp.bfloat16), RIGHT)
    rank_cols = mm(identity, jnp.where(present, rank, 0.0).astype(jnp.bfloat16), RIGHT)
    z_slot = z_slot_of(iota((128, 1), 0) // PLANE)
    plane_base = (CAPACITY * z_slot).astype(jnp.float32) + 1.0
    slot_lane = iota((1, n_slots), 1).astype(jnp.float32)
    found = jnp.zeros((128, n_slots), jnp.float32)
    for j in range(IMG_MAX):
        found = found + jnp.where(
            slot_cols[:, j : j + 1] == slot_lane, rank_cols[:, j : j + 1] + plane_base, 0.0
        )
    goes_to = jnp.sum(found, axis=0, keepdims=True) - 1.0
    pick1[...] = flag(iota((PLANES * CAPACITY, n_slots), 0).astype(jnp.float32) == goes_to)

    lane = iota((1, HEAD_SIZE), 1)
    first_t = jnp.zeros((1, HEAD_SIZE), jnp.int32)
    last_t = jnp.zeros((1, HEAD_SIZE), jnp.int32)
    for j in range(IMG_MAX):
        first_t = jnp.where(lane == j, pos_ref[0, j], first_t)
        last_t = jnp.where(lane == j, end_ref[0, j], last_t)
    block = iota((4 * tokens, HEAD_SIZE), 0) // (2 * tokens)
    owner = jnp.where(block == 0, core, sibling)
    t_pos = owner * tokens + iota((4 * tokens, HEAD_SIZE), 0) % tokens
    attends = (lane < count_ref[0]) & (first_t <= t_pos) & (t_pos < last_t)
    q_tail[...] = flag(jnp.logical_not(attends))
    n_keys = k_tail.shape[0]
    k_tail[...] = jnp.where(
        iota((n_keys, HEAD_SIZE), 1) == iota((n_keys, HEAD_SIZE), 0) % IMG_MAX, MASKED, 0.0
    ).astype(jnp.bfloat16)

    for i in range(4):
        x_copy(i).wait()
    for c in range(PIECES):
        cols = pl.ds(c * piece, piece)
        for i, (w, total) in enumerate(((wk_v, sum_k), (wv_v, sum_v))):
            w_copy(i, c).wait()
            if c + AHEAD < PIECES:
                w_copy(i, c + AHEAD).start()
            elif c + AHEAD == PIECES and i == 0:
                q_copy.start()
            term = mm(x_v[:, cols], w[cols, :])
            total[...] = term if c == 0 else total[...] + term

    def part_copy(i):
        total, got = ((sum_k, got_k), (sum_v, got_v))[i]
        return pltpu.make_async_remote_copy(
            src_ref=total.at[:, sib_half],
            dst_ref=got,
            send_sem=part_sems.at[0, i],
            recv_sem=part_sems.at[1, i],
            device_id=(doc, sibling),
            device_id_type=MESH,
        )

    pl.semaphore_wait(barrier, PLANES - 1 + 2 * (SIDE - 1) + 1)
    part_copy(0).start()
    part_copy(1).start()

    q_copy.wait()
    q_gain = qg_ref[...]
    half_width = QUERY_HEADS // 2 * HEAD_SIZE

    def norm_queries(n, carry):
        for u in range(4):
            i = n * 4 + u
            at = pl.multiple_of(i * HEAD_SIZE, HEAD_SIZE)
            own_cols = pl.ds(pl.multiple_of(core * half_width + at, HEAD_SIZE), HEAD_SIZE)
            sib_cols = pl.ds(pl.multiple_of(sibling * half_width + at, HEAD_SIZE), HEAD_SIZE)
            q_own[i] = head_norm(q_v[:, own_cols].astype(jnp.float32), q_gain).astype(jnp.bfloat16)
            q_send[i] = head_norm(q_v[:, sib_cols].astype(jnp.float32), q_gain).astype(jnp.bfloat16)
        return carry

    lax.fori_loop(0, QUERY_HEADS // 8, norm_queries, 0)
    q_exchange = pltpu.make_async_remote_copy(
        src_ref=q_send,
        dst_ref=q_sib,
        send_sem=q_sems.at[0],
        recv_sem=q_sems.at[1],
        device_id=(doc, sibling),
        device_id_type=MESH,
    )

    q_exchange.start()

    def hop1(s):
        return pltpu.make_async_remote_copy(
            src_ref=send1.at[s],
            dst_ref=recv1.at[own_slot],
            send_sem=s1_sem.at[s],
            recv_sem=r1_sem.at[own_slot],
            device_id=(Z_ORDER[s] * PLANE + p, core),
            device_id_type=MESH,
        )

    def hop1_in(s):
        return pltpu.make_async_remote_copy(
            src_ref=send1.at[s],
            dst_ref=recv1.at[s],
            send_sem=s1_sem.at[s],
            recv_sem=r1_sem.at[s],
            device_id=(Z_ORDER[s] * PLANE + p, core),
            device_id_type=MESH,
        )

    def if_other(s, act):
        pl.when(own_slot != s)(act)

    def hop2(k, i):
        return pltpu.make_async_remote_copy(
            src_ref=send2.at[k, i],
            dst_ref=recv2.at[k, i],
            send_sem=s2_sem.at[k],
            recv_sem=r2_sem.at[k],
            device_id=(z * PLANE + along_b(i), core),
            device_id_type=MESH,
        )

    def hop_a(k, i):
        return pltpu.make_async_remote_copy(
            src_ref=send_a.at[k, i],
            dst_ref=recv_a.at[k, i],
            send_sem=sa_sem.at[k],
            recv_sem=ra_sem.at[k],
            device_id=(z * PLANE + along_a(i), core),
            device_id_type=MESH,
        )

    def await_group(ref, k, sem):
        part = ref.at[k, pl.ds(1, SIDE - 1)]
        pltpu.make_async_copy(part, part, sem.at[k]).wait()

    key_gain = kg_ref[...]
    part_copy(0).wait_recv()
    raw_k = sum_k[:, own_half] + got_k[...]
    keys_own = [head_norm(raw_k[:, h * HEAD_SIZE : (h + 1) * HEAD_SIZE], key_gain).astype(jnp.bfloat16) for h in range(2)]
    part_copy(1).wait_recv()
    raw_v = (sum_v[:, own_half] + got_v[...]).astype(jnp.bfloat16)
    kv_own = jnp.concatenate(keys_own + [raw_v], axis=1)
    packed = mm(pick1[...], kv_own).astype(jnp.bfloat16).reshape(PLANES, CAPACITY, 2 * half)
    send1[...] = packed
    for s in range(PLANES):
        if_other(s, lambda s=s: hop1(s).start())
    recv1[own_slot] = send1[own_slot]
    def a_of(doc_ids):
        return jnp.where(core == 0, doc_ids % PLANE // SIDE, doc_ids % SIDE)

    group_rank = rank_within(same & (a_of(d_row) == a_of(d_col)))
    d_lane = iota((1, 128), 1)
    a_step = (a_of(d_lane) + SIDE - a) % SIDE
    rows_p, cols_p = SIDE * 2 * GROUP_CAPACITY, 2 * CAPACITY
    row_p = iota((rows_p, 1), 0)
    row_key = (row_p // (2 * GROUP_CAPACITY) * GROUP_CAPACITY + row_p % GROUP_CAPACITY).astype(jnp.float32)
    entry_key = jnp.where(
        present & (d_lane // PLANE == z), (a_step * GROUP_CAPACITY).astype(jnp.float32) + group_rank, -1.0
    )
    hits = jnp.zeros((rows_p, 128), jnp.float32)
    for j in range(IMG_MAX):
        hits = hits + jnp.where(entry_key[j : j + 1] == row_key, rank[j : j + 1] + 1.0, 0.0)
    plane_rank = jnp.sum(hits, axis=1, keepdims=True)
    source = (CAPACITY * (row_p // GROUP_CAPACITY % 2)).astype(jnp.float32)
    row_target = jnp.where(plane_rank > 0.0, plane_rank - 1.0 + source, -1.0)
    pick2[...] = flag(iota((rows_p, cols_p), 1).astype(jnp.float32) == row_target)

    per_step = 2 * SIDE * IMG_MAX
    rows_e, cols_e = SIDE * per_step, 2 * SIDE * GROUP_CAPACITY
    row_doc = z * PLANE + a * step_a + (b + iota((rows_e, 128), 0) // per_step) % SIDE * step_b
    mine_doc = flag(iota((rows_e, 128), 1) == row_doc)
    rank_plus = jnp.where(present, group_rank + 1.0, 0.0).astype(jnp.bfloat16)
    by_slot = mm(mine_doc, rank_plus, RIGHT)
    chosen = iota((rows_e, IMG_MAX), 1) == iota((rows_e, IMG_MAX), 0) % IMG_MAX
    row_rank = jnp.sum(jnp.where(chosen, by_slot, 0.0), axis=1, keepdims=True)
    source = (iota((rows_e, 1), 0) // IMG_MAX) % (2 * SIDE)
    row_target = jnp.where(row_rank > 0.0, row_rank - 1.0 + (GROUP_CAPACITY * source).astype(jnp.float32), -1.0)
    expand[...] = flag(iota((rows_e, cols_e), 1).astype(jnp.float32) == row_target)

    def pick_and_send(k):
        for s in (2 * k, 2 * k + 1):
            if_other(s, lambda s=s: hop1_in(s).wait_recv())
        rows = mm(pick2[...], recv1[pl.ds(2 * k, 2)].reshape(2 * CAPACITY, 2 * half)).astype(jnp.bfloat16)
        rows = rows.reshape(SIDE, 2 * GROUP_CAPACITY, 2 * half)
        recv_a[k, 0] = rows[0]
        send_a[k, pl.ds(1, SIDE - 1)] = rows[1:]
        for i in range(1, SIDE):
            hop_a(k, i).start()

    def expand_and_send(k):
        await_group(recv_a, k, ra_sem)
        rows = mm(expand[...], recv_a[k].reshape(cols_e, 2 * half)).astype(jnp.bfloat16)
        rows = rows.reshape(SIDE, per_step, 2 * half)
        recv2[k, 0] = rows[0]
        send2[k, pl.ds(1, SIDE - 1)] = rows[1:]
        for i in range(1, SIDE):
            hop2(k, i).start()

    ones = jnp.ones((n_keys, HEAD_SIZE), jnp.bfloat16)
    scale = 1.0 / math.sqrt(HEAD_SIZE)
    last = PLANES // 2 - 1

    blocks = GROUP
    per_head = blocks // 2

    def attend(k):
        await_group(recv2, k, r2_sem)

        def keys_of(b):
            at = (b // per_head) * HEAD_SIZE
            rows = recv2[k, :, :, at : at + HEAD_SIZE].reshape(n_keys, HEAD_SIZE)
            return jnp.concatenate([rows, k_tail[...]], axis=1)

        def values_of(b):
            at = half + (b // per_head) * HEAD_SIZE
            rows = recv2[k, :, :, at : at + HEAD_SIZE].reshape(n_keys, HEAD_SIZE)
            return jnp.concatenate([rows, ones], axis=1)

        def scores_of(b):
            own = q_own[2 * b : 2 * b + 2].reshape(2 * tokens, HEAD_SIZE)
            sib = q_sib[2 * b : 2 * b + 2].reshape(2 * tokens, HEAD_SIZE)
            rows = jnp.concatenate([jnp.concatenate([own, sib], axis=0), q_tail[...]], axis=1)
            return mm(rows, keys_of(b), RIGHT)

        scores = scores_of(0)
        for b in range(blocks):
            weights = jnp.exp(scores * scale).astype(jnp.bfloat16)
            if b + 1 < blocks:
                scores = scores_of(b + 1)
            mixed = mm(weights, values_of(b))
            if k > 0:
                mixed = mixed + o_sum[b]
            if k < last:
                o_sum[b] = mixed
                continue
            total = mixed[:, HEAD_SIZE:]
            out = (mixed[:, :HEAD_SIZE] / jnp.where(total > 0.0, total, 1.0)).astype(jnp.bfloat16)
            for i in range(2):
                at = (2 * b + i) * HEAD_SIZE
                o_own[:, at : at + HEAD_SIZE] = out[i * tokens : (i + 1) * tokens]
                o_send[:, at : at + HEAD_SIZE] = out[(2 + i) * tokens : (3 + i) * tokens]
            if b % 2 == 1:
                o_copy(b // 2).start()
                own_copy(b // 2).start()

    quarters = 4
    out_width = width // 2 // quarters

    def out_at(of, h):
        return out_hbm.at[:, pl.ds(pl.multiple_of((of * quarters + h) * out_width, out_width), out_width)]

    def o_copy(h):
        return pltpu.make_async_remote_copy(
            src_ref=o_send.at[:, pl.ds(h * out_width, out_width)],
            dst_ref=out_at(core, h),
            send_sem=o_sems.at[0, h],
            recv_sem=o_sems.at[1, h],
            device_id=(doc, sibling),
            device_id_type=MESH,
        )

    def o_in(h):
        return pltpu.make_async_remote_copy(
            src_ref=o_send.at[:, pl.ds(h * out_width, out_width)],
            dst_ref=out_at(sibling, h),
            send_sem=o_sems.at[0, h],
            recv_sem=o_sems.at[1, h],
            device_id=(doc, sibling),
            device_id_type=MESH,
        )

    def own_copy(h):
        return pltpu.make_async_copy(o_own.at[:, pl.ds(h * out_width, out_width)], out_at(core, h), out_sem.at[h])

    pick_and_send(0)
    pick_and_send(1)
    expand_and_send(0)
    pick_and_send(2)
    expand_and_send(1)
    q_exchange.wait_recv()
    attend(0)
    pick_and_send(3)
    expand_and_send(2)
    attend(1)
    expand_and_send(3)
    attend(2)
    attend(3)

    for i in range(2):
        part_copy(i).wait_send()
    for s in range(PLANES):
        if_other(s, lambda s=s: hop1(s).wait_send())
    for k in range(last + 1):
        await_group(send_a, k, sa_sem)
        await_group(send2, k, s2_sem)
    q_exchange.wait_send()
    for h in range(quarters):
        o_copy(h).wait_send()
        own_copy(h).wait()
        o_in(h).wait_recv()


def packed_route(
    queries,
    vision,
    key_matrix,
    value_matrix,
    query_gain,
    key_gain,
    image_count,
    image_slot,
    image_pos,
    span_end,
):
    tokens, width = queries.shape
    n_slots = vision.shape[0]
    depth = vision.shape[2]
    two = 2 * HEAD_SIZE
    anywhere = pl.BlockSpec(memory_space=pl.ANY)
    vmem = pl.BlockSpec(memory_space=pltpu.VMEM)
    smem = pl.BlockSpec(memory_space=pltpu.SMEM)
    bf16, f32 = jnp.bfloat16, jnp.float32
    dma = pltpu.SemaphoreType.DMA
    groups = PLANES // 2
    keys = 2 * PLANE * IMG_MAX
    out = pl.pallas_call(
        fused_kernel,
        out_shape=jax.ShapeDtypeStruct((tokens, width), bf16),
        in_specs=[anywhere, anywhere, anywhere, anywhere, vmem, vmem, smem, vmem, smem, smem],
        out_specs=anywhere,
        scratch_shapes=[
            pltpu.VMEM((tokens, width), bf16),
            pltpu.VMEM((n_slots, depth), bf16),
            pltpu.VMEM(key_matrix.shape, bf16),
            pltpu.VMEM(value_matrix.shape, bf16),
            pltpu.VMEM((n_slots, 2 * two), f32),
            pltpu.VMEM((n_slots, 2 * two), f32),
            pltpu.VMEM((n_slots, two), f32),
            pltpu.VMEM((n_slots, two), f32),
            pltpu.VMEM((PLANES * CAPACITY, n_slots), bf16),
            pltpu.VMEM((SIDE * 2 * GROUP_CAPACITY, 2 * CAPACITY), bf16),
            pltpu.VMEM((keys, 2 * SIDE * GROUP_CAPACITY), bf16),
            pltpu.VMEM((PLANES, CAPACITY, 2 * two), bf16),
            pltpu.VMEM((PLANES, CAPACITY, 2 * two), bf16),
            pltpu.VMEM((groups, SIDE, 2 * GROUP_CAPACITY, 2 * two), bf16),
            pltpu.VMEM((groups, SIDE, 2 * GROUP_CAPACITY, 2 * two), bf16),
            pltpu.VMEM((groups, SIDE, keys // SIDE, 2 * two), bf16),
            pltpu.VMEM((groups, SIDE, keys // SIDE, 2 * two), bf16),
            pltpu.VMEM((QUERY_HEADS // 2, tokens, HEAD_SIZE), bf16),
            pltpu.VMEM((QUERY_HEADS // 2, tokens, HEAD_SIZE), bf16),
            pltpu.VMEM((QUERY_HEADS // 2, tokens, HEAD_SIZE), bf16),
            pltpu.VMEM((4 * tokens, HEAD_SIZE), bf16),
            pltpu.VMEM((keys, HEAD_SIZE), bf16),
            pltpu.VMEM((GROUP, 4 * tokens, two), f32),
            pltpu.VMEM((tokens, width // 2), bf16),
            pltpu.VMEM((tokens, width // 2), bf16),
            dma((5,)),
            dma((2, PIECES)),
            dma((4,)),
            dma((2, 2)),
            dma((2,)),
            dma((2, 4)),
            dma((PLANES,)),
            dma((PLANES,)),
            dma((groups,)),
            dma((groups,)),
            dma((groups,)),
            dma((groups,)),
        ],
        compiler_params=pltpu.CompilerParams(
            collective_id=0, has_side_effects=True, vmem_limit_bytes=56 * 1024 * 1024
        ),
        name="fused_cross_attention",
    )(
        queries,
        vision.reshape(n_slots, depth),
        key_matrix,
        value_matrix,
        query_gain.reshape(1, HEAD_SIZE),
        key_gain.reshape(1, HEAD_SIZE),
        image_count,
        image_slot.T,
        image_pos,
        span_end,
    )
    return out


def fits_kernel(slot_ref, fits_ref):
    row, col = iota((128, 128), 0), iota((128, 128), 1)
    there = flag(slot_ref[...] >= 0)
    plane = row // PLANE == col // PLANE

    def crowd(same):
        return jnp.max(jnp.sum(mm(there, flag(same)), axis=0, keepdims=True))

    in_plane = crowd(plane)
    in_row = crowd(row // SIDE == col // SIDE)
    in_column = crowd(plane & (row % SIDE == col % SIDE))
    fits = (in_plane <= CAPACITY) & (in_row <= GROUP_CAPACITY) & (in_column <= GROUP_CAPACITY)
    fits_ref[0] = jnp.where(fits, 1, 0)


def shards(*arrays):
    image_slot = arrays[7]
    fits = pl.pallas_call(
        fits_kernel,
        out_shape=jax.ShapeDtypeStruct((1,), jnp.int32),
        in_specs=[pl.BlockSpec(memory_space=pltpu.VMEM)],
        out_specs=pl.BlockSpec(memory_space=pltpu.SMEM),
        name="fits",
    )(image_slot.T)
    return lax.cond(fits[0] > 0, packed_route, general_route, *arrays)

def solution(mesh):
    in_specs = (
        P(("doc", "seq"), None),
        P(None, "doc", "seq"),
        P("seq", None),
        P("seq", None),
        P(),
        P(),
        P("doc"),
        P(),
        P("doc", None),
        P("doc", None),
    )
    out_specs = P(("doc", "seq"), None)
    return jax.shard_map(shards, mesh=mesh, in_specs=in_specs, out_specs=out_specs, check_vma=False)
```

```python
import functools
import math

import jax
import jax.numpy as jnp
from jax import lax
from jax.experimental import pallas as pl
from jax.experimental.pallas import tpu as pltpu
from jax.sharding import PartitionSpec as P

HEAD_SIZE = 128
QUERY_HEADS = 32
KEY_VALUE_HEADS = 4
IMG_MAX = 8
GROUP = QUERY_HEADS // KEY_VALUE_HEADS
PLANE = 16
PLANES = 8
CAPACITY = 48
MESH = pl.DeviceIdType.MESH
MASKED = -32768.0
PIECES = 8
AHEAD = 3
Z_STEPS = (0, 1, 7, 2, 6, 3, 5, 4)

epsilon = 1e-05


def head_norm(values, scales):
    mean_square = jnp.mean(values * values, axis=-1, keepdims=True)
    return values * lax.rsqrt(mean_square + epsilon) * scales


def general_route(
    queries,
    vision,
    key_matrix,
    value_matrix,
    query_gain,
    key_gain,
    image_count,
    image_slot,
    image_pos,
    span_end,
):
    n_slots = vision.shape[0]
    core = lax.axis_index("seq")
    rows = vision.reshape(n_slots, -1)
    keys = jnp.dot(rows, key_matrix, preferred_element_type=jnp.float32)
    values = jnp.dot(rows, value_matrix, preferred_element_type=jnp.float32)
    half = keys.shape[1] // 2
    other = [(0, 1), (1, 0)]

    def pick(c):
        start = c * half
        return jnp.concatenate(
            [lax.dynamic_slice_in_dim(keys, start, half, 1), lax.dynamic_slice_in_dim(values, start, half, 1)], axis=1
        )

    mine = pick(core) + lax.ppermute(pick(1 - core), "seq", other)
    mine = mine.reshape(n_slots, 2, 2, HEAD_SIZE)
    kv = jnp.concatenate(
        [head_norm(mine[:, 0], key_gain).astype(jnp.bfloat16), mine[:, 1].astype(jnp.bfloat16)], axis=1
    ).reshape(n_slots, 4 * HEAD_SIZE)
    slots = image_slot.reshape(-1)
    one_hot = (slots[:, None] == jnp.arange(n_slots, dtype=jnp.int32)[None, :]).astype(jnp.bfloat16)
    packed = jnp.dot(one_hot, kv, preferred_element_type=jnp.float32).astype(jnp.bfloat16)
    packed = packed.reshape(image_slot.shape[0], IMG_MAX * 4 * HEAD_SIZE)
    got = lax.all_to_all(packed, "doc", split_axis=0, concat_axis=0, tiled=True)
    theirs = lax.ppermute(got, "seq", other)
    first = jnp.where(core == 0, got, theirs).reshape(-1, IMG_MAX, 2, 2, HEAD_SIZE)
    second = jnp.where(core == 0, theirs, got).reshape(-1, IMG_MAX, 2, 2, HEAD_SIZE)
    both = jnp.concatenate([first, second], axis=3)
    n_keys = both.shape[0] * IMG_MAX
    both = both.reshape(n_keys, 2, KEY_VALUE_HEADS, HEAD_SIZE)
    local_tokens = queries.shape[0]
    positions = core * local_tokens + jnp.arange(local_tokens, dtype=jnp.int32)
    q = queries.astype(jnp.float32).reshape(local_tokens, KEY_VALUE_HEADS, GROUP, HEAD_SIZE)
    q = head_norm(q, query_gain).astype(jnp.bfloat16)
    seen = jnp.arange(IMG_MAX, dtype=jnp.int32)
    attends = (
        (seen[None, :] < image_count[0])
        & (image_pos[0][None, :] <= positions[:, None])
        & (positions[:, None] < span_end[0][None, :])
    )
    scores = jnp.einsum("tkgd,nkd->tkgn", q, both[:, 0], preferred_element_type=jnp.float32)
    scores = scores * (1.0 / math.sqrt(HEAD_SIZE))
    key_mask = jnp.tile(attends, (1, n_keys // IMG_MAX))
    weights = jnp.where(key_mask[:, None, None, :], jnp.exp(scores), 0.0).astype(jnp.bfloat16)
    numerator = jnp.einsum("tkgn,nkd->tkgd", weights, both[:, 1], preferred_element_type=jnp.float32)
    denominator = jnp.sum(weights, axis=3, dtype=jnp.float32)
    reached = jnp.any(attends, axis=1)[:, None, None]
    quotient = numerator / jnp.where(reached, denominator, 1.0)[..., None]
    mixed_rows = jnp.where(reached[..., None], quotient, 0.0).astype(jnp.bfloat16)
    return mixed_rows.reshape(local_tokens, QUERY_HEADS * HEAD_SIZE)


def iota(shape, axis):
    return lax.broadcasted_iota(jnp.int32, shape, axis)


def flag(condition):
    return condition.astype(jnp.float32).astype(jnp.bfloat16)


def mm(a, b, contract=((1,), (0,))):
    return lax.dot_general(a, b, (contract, ((), ())), preferred_element_type=jnp.float32)


RIGHT = ((1,), (1,))


def fused_kernel(
    q_hbm,
    x_hbm,
    wk_hbm,
    wv_hbm,
    qg_ref,
    kg_ref,
    count_ref,
    slot_ref,
    pos_ref,
    end_ref,
    out_hbm,
    q_v,
    x_v,
    wk_v,
    wv_v,
    sum_k,
    sum_v,
    got_k,
    got_v,
    pick1,
    expand,
    pick_own,
    expand_far,
    send1,
    recv1,
    send2,
    recv2,
    send_one,
    recv_one,
    q_send,
    q_own,
    q_sib,
    q_tail,
    k_tail,
    o_sum,
    o_own,
    o_send,
    local_sem,
    w_sem,
    out_sem,
    part_sems,
    q_sems,
    o_sems,
    s1_sem,
    r1_sem,
    s2_sem,
    r2_sem,
    so_sem,
    ro_sem,
):
    doc = lax.axis_index("doc")
    core = lax.axis_index("seq")
    sibling = 1 - core
    z, p = doc // PLANE, doc % PLANE
    px, py = p // 4, p % 4
    tokens, width = q_v.shape
    n_slots, depth = x_v.shape
    piece = depth // PIECES
    row_block = n_slots // 4
    half = KEY_VALUE_HEADS // 2 * HEAD_SIZE
    own_half = pl.ds(pl.multiple_of(core * half, half), half)
    sib_half = pl.ds(pl.multiple_of(sibling * half, half), half)

    def x_copy(i):
        rows = pl.ds(i * row_block, row_block)
        return pltpu.make_async_copy(x_hbm.at[rows], x_v.at[rows], local_sem.at[i])

    q_copy = pltpu.make_async_copy(q_hbm, q_v, local_sem.at[4])

    def w_copy(i, c):
        rows = pl.ds(c * piece, piece)
        hbm, v = ((wk_hbm, wk_v), (wv_hbm, wv_v))[i]
        return pltpu.make_async_copy(hbm.at[rows], v.at[rows], w_sem.at[i, c])

    for i in range(4):
        x_copy(i).start()
    for c in range(AHEAD):
        w_copy(0, c).start()
        w_copy(1, c).start()

    def z_to(s):
        return (z + Z_STEPS[s]) % PLANES

    def plane_to(i):
        return ((px + i // 4) % 4) * 4 + (py + i % 4) % 4

    barrier = pltpu.get_barrier_semaphore()
    pl.semaphore_signal(barrier, inc=1, device_id=(doc, sibling), device_id_type=MESH)

    def greet_z(i, carry):
        there = ((z + i) % PLANES) * PLANE + p
        pl.semaphore_signal(barrier, inc=1, device_id=(there, core), device_id_type=MESH)
        return carry

    def greet_plane(i, carry):
        pl.semaphore_signal(barrier, inc=1, device_id=(z * PLANE + plane_to(i), core), device_id_type=MESH)
        return carry

    lax.fori_loop(1, PLANES, greet_z, 0)
    lax.fori_loop(1, PLANE, greet_plane, 0)

    slots_t = slot_ref[...]
    present = slots_t >= 0
    there = flag(present)
    d_row, d_col = iota((128, 128), 0), iota((128, 128), 1)
    same = (d_row // PLANE) == (d_col // PLANE)
    before = mm(there, flag(same & (d_row < d_col)))
    totals = mm(there, flag(same)).astype(jnp.bfloat16)
    earlier = mm(flag(iota((8, 8), 1) < iota((8, 8), 0)), totals)
    rank = before + earlier
    identity = flag(d_row == d_col)
    slot_cols = mm(identity, slots_t.astype(jnp.float32).astype(jnp.bfloat16), RIGHT)
    rank_cols = mm(identity, jnp.where(present, rank, 0.0).astype(jnp.bfloat16), RIGHT)
    away = (iota((128, 1), 0) // PLANE + PLANES - z) % PLANES
    z_slot = jnp.where(away == 0, 0, jnp.where(away <= PLANES // 2, 2 * away - 1, 2 * (PLANES - away)))
    plane_base = (CAPACITY * z_slot).astype(jnp.float32) + 1.0
    slot_lane = iota((1, n_slots), 1).astype(jnp.float32)
    found = jnp.zeros((128, n_slots), jnp.float32)
    for j in range(IMG_MAX):
        found = found + jnp.where(
            slot_cols[:, j : j + 1] == slot_lane, rank_cols[:, j : j + 1] + plane_base, 0.0
        )
    goes_to = jnp.sum(found, axis=0, keepdims=True) - 1.0
    pick1[...] = flag(iota((PLANES * CAPACITY, n_slots), 0).astype(jnp.float32) == goes_to)

    def by_document(entries, rows, per_document):
        step = iota((rows, 128), 0) // per_document
        row_doc = z * PLANE + ((px + step // 4) % 4) * 4 + (py + step % 4) % 4
        by_slot = mm(flag(iota((rows, 128), 1) == row_doc), entries.astype(jnp.bfloat16), RIGHT)
        chosen = iota((rows, IMG_MAX), 1) == iota((rows, IMG_MAX), 0) % IMG_MAX
        return jnp.sum(jnp.where(chosen, by_slot, 0.0), axis=1, keepdims=True)

    rows_o = PLANE * IMG_MAX
    slot_plus = jnp.where(present, (slots_t + 1).astype(jnp.float32), 0.0)
    rank_plus = jnp.where(present, rank + 1.0, 0.0)
    pick_own[...] = flag(iota((rows_o, n_slots), 1).astype(jnp.float32) == by_document(slot_plus, rows_o, IMG_MAX) - 1.0)

    lane = iota((1, HEAD_SIZE), 1)
    first_t = jnp.zeros((1, HEAD_SIZE), jnp.int32)
    last_t = jnp.zeros((1, HEAD_SIZE), jnp.int32)
    for j in range(IMG_MAX):
        first_t = jnp.where(lane == j, pos_ref[0, j], first_t)
        last_t = jnp.where(lane == j, end_ref[0, j], last_t)
    block = iota((4 * tokens, HEAD_SIZE), 0) // (2 * tokens)
    owner = jnp.where(block == 0, core, sibling)
    t_pos = owner * tokens + iota((4 * tokens, HEAD_SIZE), 0) % tokens
    attends = (lane < count_ref[0]) & (first_t <= t_pos) & (t_pos < last_t)
    q_tail[...] = flag(jnp.logical_not(attends))
    n_keys = k_tail.shape[0]
    k_tail[...] = jnp.where(
        iota((n_keys, HEAD_SIZE), 1) == iota((n_keys, HEAD_SIZE), 0) % IMG_MAX, MASKED, 0.0
    ).astype(jnp.bfloat16)

    for i in range(4):
        x_copy(i).wait()
    for c in range(PIECES):
        cols = pl.ds(c * piece, piece)
        for i, (w, total) in enumerate(((wk_v, sum_k), (wv_v, sum_v))):
            w_copy(i, c).wait()
            if c + AHEAD < PIECES:
                w_copy(i, c + AHEAD).start()
            elif c + AHEAD == PIECES and i == 0:
                q_copy.start()
            term = mm(x_v[:, cols], w[cols, :])
            total[...] = term if c == 0 else total[...] + term

    def part_copy(i):
        total, got = ((sum_k, got_k), (sum_v, got_v))[i]
        return pltpu.make_async_remote_copy(
            src_ref=total.at[:, sib_half],
            dst_ref=got,
            send_sem=part_sems.at[0, i],
            recv_sem=part_sems.at[1, i],
            device_id=(doc, sibling),
            device_id_type=MESH,
        )

    pl.semaphore_wait(barrier, PLANES - 1 + PLANE - 1 + 1)
    part_copy(0).start()
    part_copy(1).start()

    q_copy.wait()
    q_gain = qg_ref[...]
    half_width = QUERY_HEADS // 2 * HEAD_SIZE

    def norm_queries(n, carry):
        for u in range(4):
            i = n * 4 + u
            at = pl.multiple_of(i * HEAD_SIZE, HEAD_SIZE)
            own_cols = pl.ds(pl.multiple_of(core * half_width + at, HEAD_SIZE), HEAD_SIZE)
            sib_cols = pl.ds(pl.multiple_of(sibling * half_width + at, HEAD_SIZE), HEAD_SIZE)
            q_own[i] = head_norm(q_v[:, own_cols].astype(jnp.float32), q_gain).astype(jnp.bfloat16)
            q_send[i] = head_norm(q_v[:, sib_cols].astype(jnp.float32), q_gain).astype(jnp.bfloat16)
        return carry

    lax.fori_loop(0, QUERY_HEADS // 8, norm_queries, 0)
    q_exchange = pltpu.make_async_remote_copy(
        src_ref=q_send,
        dst_ref=q_sib,
        send_sem=q_sems.at[0],
        recv_sem=q_sems.at[1],
        device_id=(doc, sibling),
        device_id_type=MESH,
    )

    q_exchange.start()

    def hop1(s):
        return pltpu.make_async_remote_copy(
            src_ref=send1.at[s],
            dst_ref=recv1.at[s],
            send_sem=s1_sem.at[s],
            recv_sem=r1_sem.at[s],
            device_id=(z_to(s) * PLANE + p, core),
            device_id_type=MESH,
        )

    def hop2(k, i):
        return pltpu.make_async_remote_copy(
            src_ref=send2.at[k, i],
            dst_ref=recv2.at[k, i],
            send_sem=s2_sem.at[k],
            recv_sem=r2_sem.at[k],
            device_id=(z * PLANE + plane_to(i), core),
            device_id_type=MESH,
        )

    def await_group(ref, k, sem):
        part = ref.at[k, pl.ds(1, PLANE - 1)]
        pltpu.make_async_copy(part, part, sem.at[k]).wait()

    key_gain = kg_ref[...]
    part_copy(0).wait_recv()
    raw_k = sum_k[:, own_half] + got_k[...]
    keys_own = [head_norm(raw_k[:, h * HEAD_SIZE : (h + 1) * HEAD_SIZE], key_gain).astype(jnp.bfloat16) for h in range(2)]
    part_copy(1).wait_recv()
    raw_v = (sum_v[:, own_half] + got_v[...]).astype(jnp.bfloat16)
    kv_own = jnp.concatenate(keys_own + [raw_v], axis=1)
    packed = mm(pick1[...], kv_own).astype(jnp.bfloat16).reshape(PLANES, CAPACITY, 2 * half)
    for s in range(1, PLANES):
        send1[s] = packed[s]
    for s in range(1, PLANES):
        hop1(s).start()
    def hop_one(n, i):
        return pltpu.make_async_remote_copy(
            src_ref=send_one.at[n, i],
            dst_ref=recv_one.at[n, i],
            send_sem=so_sem.at[n],
            recv_sem=ro_sem.at[n],
            device_id=(z * PLANE + plane_to(i), core),
            device_id_type=MESH,
        )

    def send_single(n, rows):
        rows = rows.reshape(PLANE, IMG_MAX, 2 * half)
        rows = jnp.concatenate([rows[:, :, :half], rows[:, :, half:]], axis=1).astype(jnp.bfloat16)
        recv_one[n, 0] = rows[0]
        send_one[n, pl.ds(1, PLANE - 1)] = rows[1:]

        def body(i, carry):
            hop_one(n, PLANE - i).start()
            return carry

        lax.fori_loop(1, PLANE, body, 0)

    send_single(0, mm(pick_own[...], kv_own))
    pair = 2 * IMG_MAX
    rows_e, cols_e = PLANE * pair, 2 * CAPACITY
    row_rank = by_document(rank_plus, rows_e, pair)
    source = (iota((rows_e, 1), 0) // IMG_MAX) % 2
    row_target = jnp.where(row_rank > 0.0, row_rank - 1.0 + (CAPACITY * source).astype(jnp.float32), -1.0)
    expand_far[...] = flag(
        iota((rows_o, CAPACITY), 1).astype(jnp.float32) == by_document(rank_plus, rows_o, IMG_MAX) - 1.0
    )
    expand[...] = flag(iota((rows_e, cols_e), 1).astype(jnp.float32) == row_target)

    def expand_and_send(k):
        for s in (2 * k + 1, 2 * k + 2):
            hop1(s).wait_recv()
        rows = mm(expand[...], recv1[pl.ds(2 * k + 1, 2)].reshape(2 * CAPACITY, 2 * half)).astype(jnp.bfloat16)
        rows = rows.reshape(PLANE, pair, 2 * half)
        recv2[k, 0] = rows[0]
        send2[k, pl.ds(1, PLANE - 1)] = rows[1:]

        def body(i, carry):
            hop2(k, PLANE - i).start()
            return carry

        lax.fori_loop(1, PLANE, body, 0)

    ones = jnp.ones((n_keys, HEAD_SIZE), jnp.bfloat16)
    scale = 1.0 / math.sqrt(HEAD_SIZE)
    last = PLANES // 2 - 1

    blocks = GROUP
    per_head = blocks // 2

    def attend(k):
        if k < last:
            await_group(recv2, k, r2_sem)
        else:
            await_group(recv_one, 0, ro_sem)
            await_group(recv_one, 1, ro_sem)
            rows = recv_one[...].astype(jnp.float32)
            keys = rows[:, :, :IMG_MAX].reshape(n_keys, half)
            values = rows[:, :, IMG_MAX:].reshape(n_keys, half)
            joined = jnp.concatenate([keys, values], axis=1).astype(jnp.bfloat16)
            recv2[k] = joined.reshape(PLANE, pair, 2 * half)

        def keys_of(b):
            at = (b // per_head) * HEAD_SIZE
            rows = recv2[k, :, :, at : at + HEAD_SIZE].reshape(n_keys, HEAD_SIZE)
            return jnp.concatenate([rows, k_tail[...]], axis=1)

        def values_of(b):
            at = half + (b // per_head) * HEAD_SIZE
            rows = recv2[k, :, :, at : at + HEAD_SIZE].reshape(n_keys, HEAD_SIZE)
            return jnp.concatenate([rows, ones], axis=1)

        def scores_of(b):
            own = q_own[2 * b : 2 * b + 2].reshape(2 * tokens, HEAD_SIZE)
            sib = q_sib[2 * b : 2 * b + 2].reshape(2 * tokens, HEAD_SIZE)
            rows = jnp.concatenate([jnp.concatenate([own, sib], axis=0), q_tail[...]], axis=1)
            return mm(rows, keys_of(b), RIGHT)

        scores = scores_of(0)
        for b in range(blocks):
            weights = jnp.exp(scores * scale).astype(jnp.bfloat16)
            if b + 1 < blocks:
                scores = scores_of(b + 1)
            mixed = mm(weights, values_of(b))
            if k > 0:
                mixed = mixed + o_sum[b]
            if k < last:
                o_sum[b] = mixed
                continue
            total = mixed[:, HEAD_SIZE:]
            out = (mixed[:, :HEAD_SIZE] / jnp.where(total > 0.0, total, 1.0)).astype(jnp.bfloat16)
            for i in range(2):
                at = (2 * b + i) * HEAD_SIZE
                o_own[:, at : at + HEAD_SIZE] = out[i * tokens : (i + 1) * tokens]
                o_send[:, at : at + HEAD_SIZE] = out[(2 + i) * tokens : (3 + i) * tokens]
            if b % 2 == 1:
                o_copy(b // 2).start()
                own_copy(b // 2).start()

    quarters = 4
    out_width = width // 2 // quarters

    def out_at(of, h):
        return out_hbm.at[:, pl.ds(pl.multiple_of((of * quarters + h) * out_width, out_width), out_width)]

    def o_copy(h):
        return pltpu.make_async_remote_copy(
            src_ref=o_send.at[:, pl.ds(h * out_width, out_width)],
            dst_ref=out_at(core, h),
            send_sem=o_sems.at[0, h],
            recv_sem=o_sems.at[1, h],
            device_id=(doc, sibling),
            device_id_type=MESH,
        )

    def o_in(h):
        return pltpu.make_async_remote_copy(
            src_ref=o_send.at[:, pl.ds(h * out_width, out_width)],
            dst_ref=out_at(sibling, h),
            send_sem=o_sems.at[0, h],
            recv_sem=o_sems.at[1, h],
            device_id=(doc, sibling),
            device_id_type=MESH,
        )

    def own_copy(h):
        return pltpu.make_async_copy(o_own.at[:, pl.ds(h * out_width, out_width)], out_at(core, h), out_sem.at[h])

    expand_and_send(0)
    expand_and_send(1)
    q_exchange.wait_recv()
    expand_and_send(2)
    attend(0)
    hop1(PLANES - 1).wait_recv()
    send_single(1, mm(expand_far[...], recv1[PLANES - 1]))
    attend(1)
    attend(2)
    attend(3)

    for i in range(2):
        part_copy(i).wait_send()
    for s in range(1, PLANES):
        hop1(s).wait_send()
    for k in range(last):
        await_group(send2, k, s2_sem)
    await_group(send_one, 0, so_sem)
    await_group(send_one, 1, so_sem)
    q_exchange.wait_send()
    for h in range(quarters):
        o_copy(h).wait_send()
        own_copy(h).wait()
        o_in(h).wait_recv()


def packed_route(
    queries,
    vision,
    key_matrix,
    value_matrix,
    query_gain,
    key_gain,
    image_count,
    image_slot,
    image_pos,
    span_end,
):
    tokens, width = queries.shape
    n_slots = vision.shape[0]
    depth = vision.shape[2]
    two = 2 * HEAD_SIZE
    anywhere = pl.BlockSpec(memory_space=pl.ANY)
    vmem = pl.BlockSpec(memory_space=pltpu.VMEM)
    smem = pl.BlockSpec(memory_space=pltpu.SMEM)
    bf16, f32 = jnp.bfloat16, jnp.float32
    dma = pltpu.SemaphoreType.DMA
    groups = PLANES // 2
    pair = 2 * IMG_MAX
    out = pl.pallas_call(
        fused_kernel,
        out_shape=jax.ShapeDtypeStruct((tokens, width), bf16),
        in_specs=[anywhere, anywhere, anywhere, anywhere, vmem, vmem, smem, vmem, smem, smem],
        out_specs=anywhere,
        scratch_shapes=[
            pltpu.VMEM((tokens, width), bf16),
            pltpu.VMEM((n_slots, depth), bf16),
            pltpu.VMEM(key_matrix.shape, bf16),
            pltpu.VMEM(value_matrix.shape, bf16),
            pltpu.VMEM((n_slots, 2 * two), f32),
            pltpu.VMEM((n_slots, 2 * two), f32),
            pltpu.VMEM((n_slots, two), f32),
            pltpu.VMEM((n_slots, two), f32),
            pltpu.VMEM((PLANES * CAPACITY, n_slots), bf16),
            pltpu.VMEM((PLANE * pair, 2 * CAPACITY), bf16),
            pltpu.VMEM((PLANE * IMG_MAX, n_slots), bf16),
            pltpu.VMEM((PLANE * IMG_MAX, CAPACITY), bf16),
            pltpu.VMEM((PLANES, CAPACITY, 2 * two), bf16),
            pltpu.VMEM((PLANES, CAPACITY, 2 * two), bf16),
            pltpu.VMEM((groups, PLANE, pair, 2 * two), bf16),
            pltpu.VMEM((groups, PLANE, pair, 2 * two), bf16),
            pltpu.VMEM((2, PLANE, pair, two), bf16),
            pltpu.VMEM((2, PLANE, pair, two), bf16),
            pltpu.VMEM((QUERY_HEADS // 2, tokens, HEAD_SIZE), bf16),
            pltpu.VMEM((QUERY_HEADS // 2, tokens, HEAD_SIZE), bf16),
            pltpu.VMEM((QUERY_HEADS // 2, tokens, HEAD_SIZE), bf16),
            pltpu.VMEM((4 * tokens, HEAD_SIZE), bf16),
            pltpu.VMEM((PLANE * pair, HEAD_SIZE), bf16),
            pltpu.VMEM((GROUP, 4 * tokens, two), f32),
            pltpu.VMEM((tokens, width // 2), bf16),
            pltpu.VMEM((tokens, width // 2), bf16),
            dma((5,)),
            dma((2, PIECES)),
            dma((4,)),
            dma((2, 2)),
            dma((2,)),
            dma((2, 4)),
            dma((PLANES,)),
            dma((PLANES,)),
            dma((groups,)),
            dma((groups,)),
            dma((2,)),
            dma((2,)),
        ],
        compiler_params=pltpu.CompilerParams(
            collective_id=0, has_side_effects=True, vmem_limit_bytes=56 * 1024 * 1024
        ),
        name="fused_cross_attention",
    )(
        queries,
        vision.reshape(n_slots, depth),
        key_matrix,
        value_matrix,
        query_gain.reshape(1, HEAD_SIZE),
        key_gain.reshape(1, HEAD_SIZE),
        image_count,
        image_slot.T,
        image_pos,
        span_end,
    )
    return out


def fits_kernel(slot_ref, fits_ref):
    same = (iota((128, 128), 0) // PLANE) == (iota((128, 128), 1) // PLANE)
    totals = mm(flag(slot_ref[...] >= 0), flag(same))
    crowded = jnp.max(jnp.sum(totals, axis=0, keepdims=True))
    fits_ref[0] = jnp.where(crowded <= CAPACITY, 1, 0)


def shards(*arrays):
    image_slot = arrays[7]
    fits = pl.pallas_call(
        fits_kernel,
        out_shape=jax.ShapeDtypeStruct((1,), jnp.int32),
        in_specs=[pl.BlockSpec(memory_space=pltpu.VMEM)],
        out_specs=pl.BlockSpec(memory_space=pltpu.SMEM),
        name="fits",
    )(image_slot.T)
    return lax.cond(fits[0] > 0, packed_route, general_route, *arrays)

def solution(mesh):
    in_specs = (
        P(("doc", "seq"), None),
        P(None, "doc", "seq"),
        P("seq", None),
        P("seq", None),
        P(),
        P(),
        P("doc"),
        P(),
        P("doc", None),
        P("doc", None),
    )
    out_specs = P(("doc", "seq"), None)
    return jax.shard_map(shards, mesh=mesh, in_specs=in_specs, out_specs=out_specs, check_vma=False)
```

```python
import functools
import math

import jax
import jax.numpy as jnp
from jax import lax
from jax.experimental import pallas as pl
from jax.experimental.pallas import tpu as pltpu
from jax.sharding import PartitionSpec as P

HEAD_SIZE = 128
QUERY_HEADS = 32
KEY_VALUE_HEADS = 4
IMG_MAX = 8
GROUP = QUERY_HEADS // KEY_VALUE_HEADS
PLANE = 16
PLANES = 8
CAPACITY = 48
MESH = pl.DeviceIdType.MESH
MASKED = -32768.0
PIECES = 8
AHEAD = 6
Z_STEPS = (0, 1, 7, 2, 6, 3, 5, 4)

epsilon = 1e-05


def head_norm(values, scales):
    mean_square = jnp.mean(values * values, axis=-1, keepdims=True)
    return values * lax.rsqrt(mean_square + epsilon) * scales


def general_route(
    queries,
    vision,
    key_matrix,
    value_matrix,
    query_gain,
    key_gain,
    image_count,
    image_slot,
    image_pos,
    span_end,
):
    n_slots = vision.shape[0]
    core = lax.axis_index("seq")
    rows = vision.reshape(n_slots, -1)
    keys = jnp.dot(rows, key_matrix, preferred_element_type=jnp.float32)
    values = jnp.dot(rows, value_matrix, preferred_element_type=jnp.float32)
    half = keys.shape[1] // 2
    other = [(0, 1), (1, 0)]

    def pick(c):
        start = c * half
        return jnp.concatenate(
            [lax.dynamic_slice_in_dim(keys, start, half, 1), lax.dynamic_slice_in_dim(values, start, half, 1)], axis=1
        )

    mine = pick(core) + lax.ppermute(pick(1 - core), "seq", other)
    mine = mine.reshape(n_slots, 2, 2, HEAD_SIZE)
    kv = jnp.concatenate(
        [head_norm(mine[:, 0], key_gain).astype(jnp.bfloat16), mine[:, 1].astype(jnp.bfloat16)], axis=1
    ).reshape(n_slots, 4 * HEAD_SIZE)
    slots = image_slot.reshape(-1)
    one_hot = (slots[:, None] == jnp.arange(n_slots, dtype=jnp.int32)[None, :]).astype(jnp.bfloat16)
    packed = jnp.dot(one_hot, kv, preferred_element_type=jnp.float32).astype(jnp.bfloat16)
    packed = packed.reshape(image_slot.shape[0], IMG_MAX * 4 * HEAD_SIZE)
    got = lax.all_to_all(packed, "doc", split_axis=0, concat_axis=0, tiled=True)
    theirs = lax.ppermute(got, "seq", other)
    first = jnp.where(core == 0, got, theirs).reshape(-1, IMG_MAX, 2, 2, HEAD_SIZE)
    second = jnp.where(core == 0, theirs, got).reshape(-1, IMG_MAX, 2, 2, HEAD_SIZE)
    both = jnp.concatenate([first, second], axis=3)
    n_keys = both.shape[0] * IMG_MAX
    both = both.reshape(n_keys, 2, KEY_VALUE_HEADS, HEAD_SIZE)
    local_tokens = queries.shape[0]
    positions = core * local_tokens + jnp.arange(local_tokens, dtype=jnp.int32)
    q = queries.astype(jnp.float32).reshape(local_tokens, KEY_VALUE_HEADS, GROUP, HEAD_SIZE)
    q = head_norm(q, query_gain).astype(jnp.bfloat16)
    seen = jnp.arange(IMG_MAX, dtype=jnp.int32)
    attends = (
        (seen[None, :] < image_count[0])
        & (image_pos[0][None, :] <= positions[:, None])
        & (positions[:, None] < span_end[0][None, :])
    )
    scores = jnp.einsum("tkgd,nkd->tkgn", q, both[:, 0], preferred_element_type=jnp.float32)
    scores = scores * (1.0 / math.sqrt(HEAD_SIZE))
    key_mask = jnp.tile(attends, (1, n_keys // IMG_MAX))
    weights = jnp.where(key_mask[:, None, None, :], jnp.exp(scores), 0.0).astype(jnp.bfloat16)
    numerator = jnp.einsum("tkgn,nkd->tkgd", weights, both[:, 1], preferred_element_type=jnp.float32)
    denominator = jnp.sum(weights, axis=3, dtype=jnp.float32)
    reached = jnp.any(attends, axis=1)[:, None, None]
    quotient = numerator / jnp.where(reached, denominator, 1.0)[..., None]
    mixed_rows = jnp.where(reached[..., None], quotient, 0.0).astype(jnp.bfloat16)
    return mixed_rows.reshape(local_tokens, QUERY_HEADS * HEAD_SIZE)


def iota(shape, axis):
    return lax.broadcasted_iota(jnp.int32, shape, axis)


def flag(condition):
    return condition.astype(jnp.float32).astype(jnp.bfloat16)


def mm(a, b, contract=((1,), (0,))):
    return lax.dot_general(a, b, (contract, ((), ())), preferred_element_type=jnp.float32)


RIGHT = ((1,), (1,))


def fused_kernel(
    q_hbm,
    x_hbm,
    wk_hbm,
    wv_hbm,
    qg_hbm,
    kg_hbm,
    count_ref,
    slot_hbm,
    pos_ref,
    end_ref,
    out_hbm,
    qg_ref,
    kg_ref,
    slot_ref,
    q_v,
    x_v,
    wk_v,
    wv_v,
    sum_k,
    sum_v,
    got_k,
    got_v,
    pick1,
    expand,
    pick_own,
    expand_far,
    send1,
    recv1,
    send2,
    recv2,
    send_one,
    recv_one,
    q_send,
    q_own,
    q_sib,
    q_tail,
    k_tail,
    o_sum,
    o_own,
    o_send,
    local_sem,
    w_sem,
    out_sem,
    part_sems,
    q_sems,
    o_sems,
    s1_sem,
    r1_sem,
    s2_sem,
    r2_sem,
    so_sem,
    ro_sem,
):
    doc = lax.axis_index("doc")
    core = lax.axis_index("seq")
    sibling = 1 - core
    z, p = doc // PLANE, doc % PLANE
    px, py = p // 4, p % 4
    tokens, width = q_v.shape
    n_slots, depth = x_v.shape
    piece = depth // PIECES
    row_block = n_slots // 4
    half = KEY_VALUE_HEADS // 2 * HEAD_SIZE
    own_half = pl.ds(pl.multiple_of(core * half, half), half)
    sib_half = pl.ds(pl.multiple_of(sibling * half, half), half)

    def x_copy(i):
        rows = pl.ds(i * row_block, row_block)
        return pltpu.make_async_copy(x_hbm.at[rows], x_v.at[rows], local_sem.at[i])

    q_copy = pltpu.make_async_copy(q_hbm, q_v, local_sem.at[4])

    def w_copy(i, c):
        rows = pl.ds(c * piece, piece)
        hbm, v = ((wk_hbm, wk_v), (wv_hbm, wv_v))[i]
        return pltpu.make_async_copy(hbm.at[rows], v.at[rows], w_sem.at[i, c])

    small = [
        pltpu.make_async_copy(slot_hbm, slot_ref, local_sem.at[5]),
        pltpu.make_async_copy(qg_hbm, qg_ref, local_sem.at[6]),
        pltpu.make_async_copy(kg_hbm, kg_ref, local_sem.at[7]),
    ]
    for copy in small:
        copy.start()
    for i in range(4):
        x_copy(i).start()
    order = [(i, c) for i in range(2) for c in range(PIECES)]
    for n in range(AHEAD):
        w_copy(*order[n]).start()

    def z_to(s):
        return (z + Z_STEPS[s]) % PLANES

    def plane_to(i):
        return ((px + i // 4) % 4) * 4 + (py + i % 4) % 4

    barrier = pltpu.get_barrier_semaphore()
    pl.semaphore_signal(barrier, inc=1, device_id=(doc, sibling), device_id_type=MESH)

    def greet_z(i, carry):
        there = ((z + i) % PLANES) * PLANE + p
        pl.semaphore_signal(barrier, inc=1, device_id=(there, core), device_id_type=MESH)
        return carry

    def greet_plane(i, carry):
        pl.semaphore_signal(barrier, inc=1, device_id=(z * PLANE + plane_to(i), core), device_id_type=MESH)
        return carry

    lax.fori_loop(1, PLANES, greet_z, 0)
    lax.fori_loop(1, PLANE, greet_plane, 0)

    for copy in small:
        copy.wait()

    slots_t = slot_ref[...]
    present = slots_t >= 0
    there = flag(present)
    d_row, d_col = iota((128, 128), 0), iota((128, 128), 1)
    same = (d_row // PLANE) == (d_col // PLANE)
    before = mm(there, flag(same & (d_row < d_col)))
    totals = mm(there, flag(same)).astype(jnp.bfloat16)
    earlier = mm(flag(iota((8, 8), 1) < iota((8, 8), 0)), totals)
    rank = before + earlier
    identity = flag(d_row == d_col)
    slot_cols = mm(identity, slots_t.astype(jnp.float32).astype(jnp.bfloat16), RIGHT)
    rank_cols = mm(identity, jnp.where(present, rank, 0.0).astype(jnp.bfloat16), RIGHT)
    away = (iota((128, 1), 0) // PLANE + PLANES - z) % PLANES
    z_slot = jnp.where(away == 0, 0, jnp.where(away <= PLANES // 2, 2 * away - 1, 2 * (PLANES - away)))
    plane_base = (CAPACITY * z_slot).astype(jnp.float32) + 1.0
    slot_lane = iota((1, n_slots), 1).astype(jnp.float32)
    found = jnp.zeros((128, n_slots), jnp.float32)
    for j in range(IMG_MAX):
        found = found + jnp.where(
            slot_cols[:, j : j + 1] == slot_lane, rank_cols[:, j : j + 1] + plane_base, 0.0
        )
    goes_to = jnp.sum(found, axis=0, keepdims=True) - 1.0
    pick1[...] = flag(iota((PLANES * CAPACITY, n_slots), 0).astype(jnp.float32) == goes_to)

    def by_document(entries, rows, per_document):
        step = iota((rows, 128), 0) // per_document
        row_doc = z * PLANE + ((px + step // 4) % 4) * 4 + (py + step % 4) % 4
        by_slot = mm(flag(iota((rows, 128), 1) == row_doc), entries.astype(jnp.bfloat16), RIGHT)
        chosen = iota((rows, IMG_MAX), 1) == iota((rows, IMG_MAX), 0) % IMG_MAX
        return jnp.sum(jnp.where(chosen, by_slot, 0.0), axis=1, keepdims=True)

    rows_o = PLANE * IMG_MAX
    slot_plus = jnp.where(present, (slots_t + 1).astype(jnp.float32), 0.0)
    rank_plus = jnp.where(present, rank + 1.0, 0.0)
    pick_own[...] = flag(iota((rows_o, n_slots), 1).astype(jnp.float32) == by_document(slot_plus, rows_o, IMG_MAX) - 1.0)

    lane = iota((1, HEAD_SIZE), 1)
    first_t = jnp.zeros((1, HEAD_SIZE), jnp.int32)
    last_t = jnp.zeros((1, HEAD_SIZE), jnp.int32)
    for j in range(IMG_MAX):
        first_t = jnp.where(lane == j, pos_ref[0, j], first_t)
        last_t = jnp.where(lane == j, end_ref[0, j], last_t)
    block = iota((4 * tokens, HEAD_SIZE), 0) // (2 * tokens)
    owner = jnp.where(block == 0, core, sibling)
    t_pos = owner * tokens + iota((4 * tokens, HEAD_SIZE), 0) % tokens
    attends = (lane < count_ref[0]) & (first_t <= t_pos) & (t_pos < last_t)
    q_tail[...] = flag(jnp.logical_not(attends))
    n_keys = k_tail.shape[0]
    k_tail[...] = jnp.where(
        iota((n_keys, HEAD_SIZE), 1) == iota((n_keys, HEAD_SIZE), 0) % IMG_MAX, MASKED, 0.0
    ).astype(jnp.bfloat16)

    def part_copy(i):
        total, got = ((sum_k, got_k), (sum_v, got_v))[i]
        return pltpu.make_async_remote_copy(
            src_ref=total.at[:, sib_half],
            dst_ref=got,
            send_sem=part_sems.at[0, i],
            recv_sem=part_sems.at[1, i],
            device_id=(doc, sibling),
            device_id_type=MESH,
        )

    for i in range(4):
        x_copy(i).wait()
    for n, (i, c) in enumerate(order):
        w, total = ((wk_v, sum_k), (wv_v, sum_v))[i]
        cols = pl.ds(c * piece, piece)
        w_copy(i, c).wait()
        if n + AHEAD < len(order):
            w_copy(*order[n + AHEAD]).start()
        elif n + AHEAD == len(order):
            q_copy.start()
        term = mm(x_v[:, cols], w[cols, :])
        total[...] = term if c == 0 else total[...] + term
        if (i, c) == (0, PIECES - 1):
            pl.semaphore_wait(barrier, PLANES - 1 + PLANE - 1 + 1)
            part_copy(0).start()
    part_copy(1).start()

    q_copy.wait()
    q_gain = qg_ref[...]
    half_width = QUERY_HEADS // 2 * HEAD_SIZE

    def norm_queries(n, carry):
        for u in range(4):
            i = n * 4 + u
            at = pl.multiple_of(i * HEAD_SIZE, HEAD_SIZE)
            own_cols = pl.ds(pl.multiple_of(core * half_width + at, HEAD_SIZE), HEAD_SIZE)
            sib_cols = pl.ds(pl.multiple_of(sibling * half_width + at, HEAD_SIZE), HEAD_SIZE)
            q_own[i] = head_norm(q_v[:, own_cols].astype(jnp.float32), q_gain).astype(jnp.bfloat16)
            q_send[i] = head_norm(q_v[:, sib_cols].astype(jnp.float32), q_gain).astype(jnp.bfloat16)
        return carry

    lax.fori_loop(0, QUERY_HEADS // 8, norm_queries, 0)
    q_exchange = pltpu.make_async_remote_copy(
        src_ref=q_send,
        dst_ref=q_sib,
        send_sem=q_sems.at[0],
        recv_sem=q_sems.at[1],
        device_id=(doc, sibling),
        device_id_type=MESH,
    )

    q_exchange.start()

    def hop1(s):
        return pltpu.make_async_remote_copy(
            src_ref=send1.at[s],
            dst_ref=recv1.at[s],
            send_sem=s1_sem.at[s],
            recv_sem=r1_sem.at[s],
            device_id=(z_to(s) * PLANE + p, core),
            device_id_type=MESH,
        )

    def hop2(k, i):
        return pltpu.make_async_remote_copy(
            src_ref=send2.at[k, i],
            dst_ref=recv2.at[k, i],
            send_sem=s2_sem.at[k],
            recv_sem=r2_sem.at[k],
            device_id=(z * PLANE + plane_to(i), core),
            device_id_type=MESH,
        )

    def await_group(ref, k, sem):
        part = ref.at[k, pl.ds(1, PLANE - 1)]
        pltpu.make_async_copy(part, part, sem.at[k]).wait()

    key_gain = kg_ref[...]
    part_copy(0).wait_recv()
    raw_k = sum_k[:, own_half] + got_k[...]
    keys_own = [head_norm(raw_k[:, h * HEAD_SIZE : (h + 1) * HEAD_SIZE], key_gain).astype(jnp.bfloat16) for h in range(2)]
    part_copy(1).wait_recv()
    raw_v = (sum_v[:, own_half] + got_v[...]).astype(jnp.bfloat16)
    kv_own = jnp.concatenate(keys_own + [raw_v], axis=1)
    packed = mm(pick1[...], kv_own).astype(jnp.bfloat16).reshape(PLANES, CAPACITY, 2 * half)
    for s in range(1, PLANES):
        send1[s] = packed[s]
    for s in range(1, PLANES):
        hop1(s).start()
    def hop_one(n, i):
        return pltpu.make_async_remote_copy(
            src_ref=send_one.at[n, i],
            dst_ref=recv_one.at[n, i],
            send_sem=so_sem.at[n],
            recv_sem=ro_sem.at[n],
            device_id=(z * PLANE + plane_to(i), core),
            device_id_type=MESH,
        )

    def send_single(n, rows):
        rows = rows.reshape(PLANE, IMG_MAX, 2 * half)
        rows = jnp.concatenate([rows[:, :, :half], rows[:, :, half:]], axis=1).astype(jnp.bfloat16)
        recv_one[n, 0] = rows[0]
        send_one[n, pl.ds(1, PLANE - 1)] = rows[1:]

        def body(i, carry):
            hop_one(n, PLANE - i).start()
            return carry

        lax.fori_loop(1, PLANE, body, 0)

    send_single(0, mm(pick_own[...], kv_own))
    pair = 2 * IMG_MAX
    rows_e, cols_e = PLANE * pair, 2 * CAPACITY
    row_rank = by_document(rank_plus, rows_e, pair)
    source = (iota((rows_e, 1), 0) // IMG_MAX) % 2
    row_target = jnp.where(row_rank > 0.0, row_rank - 1.0 + (CAPACITY * source).astype(jnp.float32), -1.0)
    expand_far[...] = flag(
        iota((rows_o, CAPACITY), 1).astype(jnp.float32) == by_document(rank_plus, rows_o, IMG_MAX) - 1.0
    )
    expand[...] = flag(iota((rows_e, cols_e), 1).astype(jnp.float32) == row_target)

    def expand_and_send(k):
        for s in (2 * k + 1, 2 * k + 2):
            hop1(s).wait_recv()
        rows = mm(expand[...], recv1[pl.ds(2 * k + 1, 2)].reshape(2 * CAPACITY, 2 * half)).astype(jnp.bfloat16)
        rows = rows.reshape(PLANE, pair, 2 * half)
        recv2[k, 0] = rows[0]
        send2[k, pl.ds(1, PLANE - 1)] = rows[1:]

        def body(i, carry):
            hop2(k, PLANE - i).start()
            return carry

        lax.fori_loop(1, PLANE, body, 0)

    ones = jnp.ones((n_keys, HEAD_SIZE), jnp.bfloat16)
    scale = 1.0 / math.sqrt(HEAD_SIZE)
    last = PLANES // 2 - 1

    blocks = GROUP
    per_head = blocks // 2

    def attend(k):
        if k < last:
            await_group(recv2, k, r2_sem)
        else:
            await_group(recv_one, 0, ro_sem)
            await_group(recv_one, 1, ro_sem)
            rows = recv_one[...].astype(jnp.float32)
            keys = rows[:, :, :IMG_MAX].reshape(n_keys, half)
            values = rows[:, :, IMG_MAX:].reshape(n_keys, half)
            joined = jnp.concatenate([keys, values], axis=1).astype(jnp.bfloat16)
            recv2[k] = joined.reshape(PLANE, pair, 2 * half)

        def keys_of(b):
            at = (b // per_head) * HEAD_SIZE
            rows = recv2[k, :, :, at : at + HEAD_SIZE].reshape(n_keys, HEAD_SIZE)
            return jnp.concatenate([rows, k_tail[...]], axis=1)

        def values_of(b):
            at = half + (b // per_head) * HEAD_SIZE
            rows = recv2[k, :, :, at : at + HEAD_SIZE].reshape(n_keys, HEAD_SIZE)
            return jnp.concatenate([rows, ones], axis=1)

        def scores_of(b):
            own = q_own[2 * b : 2 * b + 2].reshape(2 * tokens, HEAD_SIZE)
            sib = q_sib[2 * b : 2 * b + 2].reshape(2 * tokens, HEAD_SIZE)
            rows = jnp.concatenate([jnp.concatenate([own, sib], axis=0), q_tail[...]], axis=1)
            return mm(rows, keys_of(b), RIGHT)

        scores = scores_of(0)
        for b in range(blocks):
            weights = jnp.exp(scores * scale).astype(jnp.bfloat16)
            if b + 1 < blocks:
                scores = scores_of(b + 1)
            mixed = mm(weights, values_of(b))
            if k > 0:
                mixed = mixed + o_sum[b]
            if k < last:
                o_sum[b] = mixed
                continue
            total = mixed[:, HEAD_SIZE:]
            out = (mixed[:, :HEAD_SIZE] / jnp.where(total > 0.0, total, 1.0)).astype(jnp.bfloat16)
            for i in range(2):
                at = (2 * b + i) * HEAD_SIZE
                o_own[:, at : at + HEAD_SIZE] = out[i * tokens : (i + 1) * tokens]
                o_send[:, at : at + HEAD_SIZE] = out[(2 + i) * tokens : (3 + i) * tokens]
            if b % 2 == 1:
                o_copy(b // 2).start()
                own_copy(b // 2).start()

    quarters = 4
    out_width = width // 2 // quarters

    def out_at(of, h):
        return out_hbm.at[:, pl.ds(pl.multiple_of((of * quarters + h) * out_width, out_width), out_width)]

    def o_copy(h):
        return pltpu.make_async_remote_copy(
            src_ref=o_send.at[:, pl.ds(h * out_width, out_width)],
            dst_ref=out_at(core, h),
            send_sem=o_sems.at[0, h],
            recv_sem=o_sems.at[1, h],
            device_id=(doc, sibling),
            device_id_type=MESH,
        )

    def o_in(h):
        return pltpu.make_async_remote_copy(
            src_ref=o_send.at[:, pl.ds(h * out_width, out_width)],
            dst_ref=out_at(sibling, h),
            send_sem=o_sems.at[0, h],
            recv_sem=o_sems.at[1, h],
            device_id=(doc, sibling),
            device_id_type=MESH,
        )

    def own_copy(h):
        return pltpu.make_async_copy(o_own.at[:, pl.ds(h * out_width, out_width)], out_at(core, h), out_sem.at[h])

    expand_and_send(0)
    expand_and_send(1)
    q_exchange.wait_recv()
    expand_and_send(2)
    attend(0)
    hop1(PLANES - 1).wait_recv()
    send_single(1, mm(expand_far[...], recv1[PLANES - 1]))
    attend(1)
    attend(2)
    attend(3)

    for i in range(2):
        part_copy(i).wait_send()
    for s in range(1, PLANES):
        hop1(s).wait_send()
    for k in range(last):
        await_group(send2, k, s2_sem)
    await_group(send_one, 0, so_sem)
    await_group(send_one, 1, so_sem)
    q_exchange.wait_send()
    for h in range(quarters):
        o_copy(h).wait_send()
        own_copy(h).wait()
        o_in(h).wait_recv()


def packed_route(
    queries,
    vision,
    key_matrix,
    value_matrix,
    query_gain,
    key_gain,
    image_count,
    image_slot,
    image_pos,
    span_end,
):
    tokens, width = queries.shape
    n_slots = vision.shape[0]
    depth = vision.shape[2]
    two = 2 * HEAD_SIZE
    anywhere = pl.BlockSpec(memory_space=pl.ANY)
    smem = pl.BlockSpec(memory_space=pltpu.SMEM)
    bf16, f32 = jnp.bfloat16, jnp.float32
    dma = pltpu.SemaphoreType.DMA
    groups = PLANES // 2
    pair = 2 * IMG_MAX
    out = pl.pallas_call(
        fused_kernel,
        out_shape=jax.ShapeDtypeStruct((tokens, width), bf16),
        in_specs=[anywhere] * 6 + [smem, anywhere, smem, smem],
        out_specs=anywhere,
        scratch_shapes=[
            pltpu.VMEM((1, HEAD_SIZE), f32),
            pltpu.VMEM((1, HEAD_SIZE), f32),
            pltpu.VMEM((IMG_MAX, image_slot.shape[0]), jnp.int32),
            pltpu.VMEM((tokens, width), bf16),
            pltpu.VMEM((n_slots, depth), bf16),
            pltpu.VMEM(key_matrix.shape, bf16),
            pltpu.VMEM(value_matrix.shape, bf16),
            pltpu.VMEM((n_slots, 2 * two), f32),
            pltpu.VMEM((n_slots, 2 * two), f32),
            pltpu.VMEM((n_slots, two), f32),
            pltpu.VMEM((n_slots, two), f32),
            pltpu.VMEM((PLANES * CAPACITY, n_slots), bf16),
            pltpu.VMEM((PLANE * pair, 2 * CAPACITY), bf16),
            pltpu.VMEM((PLANE * IMG_MAX, n_slots), bf16),
            pltpu.VMEM((PLANE * IMG_MAX, CAPACITY), bf16),
            pltpu.VMEM((PLANES, CAPACITY, 2 * two), bf16),
            pltpu.VMEM((PLANES, CAPACITY, 2 * two), bf16),
            pltpu.VMEM((groups, PLANE, pair, 2 * two), bf16),
            pltpu.VMEM((groups, PLANE, pair, 2 * two), bf16),
            pltpu.VMEM((2, PLANE, pair, two), bf16),
            pltpu.VMEM((2, PLANE, pair, two), bf16),
            pltpu.VMEM((QUERY_HEADS // 2, tokens, HEAD_SIZE), bf16),
            pltpu.VMEM((QUERY_HEADS // 2, tokens, HEAD_SIZE), bf16),
            pltpu.VMEM((QUERY_HEADS // 2, tokens, HEAD_SIZE), bf16),
            pltpu.VMEM((4 * tokens, HEAD_SIZE), bf16),
            pltpu.VMEM((PLANE * pair, HEAD_SIZE), bf16),
            pltpu.VMEM((GROUP, 4 * tokens, two), f32),
            pltpu.VMEM((tokens, width // 2), bf16),
            pltpu.VMEM((tokens, width // 2), bf16),
            dma((8,)),
            dma((2, PIECES)),
            dma((4,)),
            dma((2, 2)),
            dma((2,)),
            dma((2, 4)),
            dma((PLANES,)),
            dma((PLANES,)),
            dma((groups,)),
            dma((groups,)),
            dma((2,)),
            dma((2,)),
        ],
        compiler_params=pltpu.CompilerParams(
            collective_id=0, has_side_effects=True, vmem_limit_bytes=56 * 1024 * 1024
        ),
        name="fused_cross_attention",
    )(
        queries,
        vision.reshape(n_slots, depth),
        key_matrix,
        value_matrix,
        query_gain.reshape(1, HEAD_SIZE),
        key_gain.reshape(1, HEAD_SIZE),
        image_count,
        image_slot.T,
        image_pos,
        span_end,
    )
    return out


def fits_kernel(slot_ref, fits_ref):
    same = (iota((128, 128), 0) // PLANE) == (iota((128, 128), 1) // PLANE)
    totals = mm(flag(slot_ref[...] >= 0), flag(same))
    crowded = jnp.max(jnp.sum(totals, axis=0, keepdims=True))
    fits_ref[0] = jnp.where(crowded <= CAPACITY, 1, 0)


def shards(*arrays):
    image_slot = arrays[7]
    fits = pl.pallas_call(
        fits_kernel,
        out_shape=jax.ShapeDtypeStruct((1,), jnp.int32),
        in_specs=[pl.BlockSpec(memory_space=pltpu.VMEM)],
        out_specs=pl.BlockSpec(memory_space=pltpu.SMEM),
        name="fits",
    )(image_slot.T)
    return lax.cond(fits[0] > 0, packed_route, general_route, *arrays)

def solution(mesh):
    in_specs = (
        P(("doc", "seq"), None),
        P(None, "doc", "seq"),
        P("seq", None),
        P("seq", None),
        P(),
        P(),
        P("doc"),
        P(),
        P("doc", None),
        P("doc", None),
    )
    out_specs = P(("doc", "seq"), None)
    return jax.shard_map(shards, mesh=mesh, in_specs=in_specs, out_specs=out_specs, check_vma=False)
```

```python
import functools
import math

import jax
import jax.numpy as jnp
from jax import lax
from jax.experimental import pallas as pl
from jax.experimental.pallas import tpu as pltpu
from jax.sharding import PartitionSpec as P

HEAD_SIZE = 128
QUERY_HEADS = 32
KEY_VALUE_HEADS = 4
IMG_MAX = 8
GROUP = QUERY_HEADS // KEY_VALUE_HEADS
PLANE = 16
PLANES = 8
CAPACITY = 48
MESH = pl.DeviceIdType.MESH
MASKED = -32768.0
PIECES = 8
AHEAD = 6
Z_STEPS = (0, 1, 7, 2, 6, 3, 5, 4)

epsilon = 1e-05


def head_norm(values, scales):
    mean_square = jnp.mean(values * values, axis=-1, keepdims=True)
    return values * lax.rsqrt(mean_square + epsilon) * scales


def general_route(
    queries,
    vision,
    key_matrix,
    value_matrix,
    query_gain,
    key_gain,
    image_count,
    image_slot,
    image_pos,
    span_end,
):
    n_slots = vision.shape[0]
    core = lax.axis_index("seq")
    rows = vision.reshape(n_slots, -1)
    keys = jnp.dot(rows, key_matrix, preferred_element_type=jnp.float32)
    values = jnp.dot(rows, value_matrix, preferred_element_type=jnp.float32)
    half = keys.shape[1] // 2
    other = [(0, 1), (1, 0)]

    def pick(c):
        start = c * half
        return jnp.concatenate(
            [lax.dynamic_slice_in_dim(keys, start, half, 1), lax.dynamic_slice_in_dim(values, start, half, 1)], axis=1
        )

    mine = pick(core) + lax.ppermute(pick(1 - core), "seq", other)
    mine = mine.reshape(n_slots, 2, 2, HEAD_SIZE)
    kv = jnp.concatenate(
        [head_norm(mine[:, 0], key_gain).astype(jnp.bfloat16), mine[:, 1].astype(jnp.bfloat16)], axis=1
    ).reshape(n_slots, 4 * HEAD_SIZE)
    slots = image_slot.reshape(-1)
    one_hot = (slots[:, None] == jnp.arange(n_slots, dtype=jnp.int32)[None, :]).astype(jnp.bfloat16)
    packed = jnp.dot(one_hot, kv, preferred_element_type=jnp.float32).astype(jnp.bfloat16)
    packed = packed.reshape(image_slot.shape[0], IMG_MAX * 4 * HEAD_SIZE)
    got = lax.all_to_all(packed, "doc", split_axis=0, concat_axis=0, tiled=True)
    theirs = lax.ppermute(got, "seq", other)
    first = jnp.where(core == 0, got, theirs).reshape(-1, IMG_MAX, 2, 2, HEAD_SIZE)
    second = jnp.where(core == 0, theirs, got).reshape(-1, IMG_MAX, 2, 2, HEAD_SIZE)
    both = jnp.concatenate([first, second], axis=3)
    n_keys = both.shape[0] * IMG_MAX
    both = both.reshape(n_keys, 2, KEY_VALUE_HEADS, HEAD_SIZE)
    local_tokens = queries.shape[0]
    positions = core * local_tokens + jnp.arange(local_tokens, dtype=jnp.int32)
    q = queries.astype(jnp.float32).reshape(local_tokens, KEY_VALUE_HEADS, GROUP, HEAD_SIZE)
    q = head_norm(q, query_gain).astype(jnp.bfloat16)
    seen = jnp.arange(IMG_MAX, dtype=jnp.int32)
    attends = (
        (seen[None, :] < image_count[0])
        & (image_pos[0][None, :] <= positions[:, None])
        & (positions[:, None] < span_end[0][None, :])
    )
    scores = jnp.einsum("tkgd,nkd->tkgn", q, both[:, 0], preferred_element_type=jnp.float32)
    scores = scores * (1.0 / math.sqrt(HEAD_SIZE))
    key_mask = jnp.tile(attends, (1, n_keys // IMG_MAX))
    weights = jnp.where(key_mask[:, None, None, :], jnp.exp(scores), 0.0).astype(jnp.bfloat16)
    numerator = jnp.einsum("tkgn,nkd->tkgd", weights, both[:, 1], preferred_element_type=jnp.float32)
    denominator = jnp.sum(weights, axis=3, dtype=jnp.float32)
    reached = jnp.any(attends, axis=1)[:, None, None]
    quotient = numerator / jnp.where(reached, denominator, 1.0)[..., None]
    mixed_rows = jnp.where(reached[..., None], quotient, 0.0).astype(jnp.bfloat16)
    return mixed_rows.reshape(local_tokens, QUERY_HEADS * HEAD_SIZE)


def iota(shape, axis):
    return lax.broadcasted_iota(jnp.int32, shape, axis)


def flag(condition):
    return condition.astype(jnp.float32).astype(jnp.bfloat16)


def mm(a, b, contract=((1,), (0,))):
    return lax.dot_general(a, b, (contract, ((), ())), preferred_element_type=jnp.float32)


RIGHT = ((1,), (1,))


def fused_kernel(
    q_hbm,
    x_hbm,
    wk_hbm,
    wv_hbm,
    qg_hbm,
    kg_hbm,
    count_ref,
    slot_hbm,
    pos_ref,
    end_ref,
    out_hbm,
    qg_ref,
    kg_ref,
    slot_ref,
    q_v,
    x_v,
    wk_v,
    wv_v,
    sum_k,
    sum_v,
    got_k,
    got_v,
    pick1,
    expand,
    pick_own,
    expand_far,
    send1,
    recv1,
    send2,
    recv2,
    send_one,
    recv_one,
    q_send,
    q_own,
    q_sib,
    q_tail,
    k_tail,
    o_sum,
    o_own,
    o_send,
    local_sem,
    w_sem,
    out_sem,
    part_sems,
    q_sems,
    o_sems,
    s1_sem,
    r1_sem,
    s2_sem,
    r2_sem,
    so_sem,
    ro_sem,
):
    doc = lax.axis_index("doc")
    core = lax.axis_index("seq")
    sibling = 1 - core
    z, p = doc // PLANE, doc % PLANE
    px, py = p // 4, p % 4
    tokens, width = q_v.shape
    n_slots, depth = x_v.shape
    piece = depth // PIECES
    row_block = n_slots // 4
    half = KEY_VALUE_HEADS // 2 * HEAD_SIZE
    own_half = pl.ds(pl.multiple_of(core * half, half), half)
    sib_half = pl.ds(pl.multiple_of(sibling * half, half), half)

    def x_copy(i):
        rows = pl.ds(i * row_block, row_block)
        return pltpu.make_async_copy(x_hbm.at[rows], x_v.at[rows], local_sem.at[i])

    q_copy = pltpu.make_async_copy(q_hbm, q_v, local_sem.at[4])

    def w_copy(i, c):
        rows = pl.ds(c * piece, piece)
        hbm, v = ((wk_hbm, wk_v), (wv_hbm, wv_v))[i]
        return pltpu.make_async_copy(hbm.at[rows], v.at[rows], w_sem.at[i, c])

    small = [
        pltpu.make_async_copy(slot_hbm, slot_ref, local_sem.at[5]),
        pltpu.make_async_copy(qg_hbm, qg_ref, local_sem.at[6]),
        pltpu.make_async_copy(kg_hbm, kg_ref, local_sem.at[7]),
    ]
    for copy in small:
        copy.start()
    for i in range(4):
        x_copy(i).start()
    order = [(i, c) for i in range(2) for c in range(PIECES)]
    for n in range(AHEAD):
        w_copy(*order[n]).start()

    def z_to(s):
        return (z + Z_STEPS[s]) % PLANES

    def plane_to(i):
        return ((px + i // 4) % 4) * 4 + (py + i % 4) % 4

    barrier = pltpu.get_barrier_semaphore()
    pl.semaphore_signal(barrier, inc=1, device_id=(doc, sibling), device_id_type=MESH)

    def greet_z(i, carry):
        there = ((z + i) % PLANES) * PLANE + p
        pl.semaphore_signal(barrier, inc=1, device_id=(there, core), device_id_type=MESH)
        return carry

    def greet_plane(i, carry):
        pl.semaphore_signal(barrier, inc=1, device_id=(z * PLANE + plane_to(i), core), device_id_type=MESH)
        return carry

    lax.fori_loop(1, PLANES, greet_z, 0)
    lax.fori_loop(1, PLANE, greet_plane, 0)

    for copy in small:
        copy.wait()

    slots_t = slot_ref[...]
    present = slots_t >= 0
    there = flag(present)
    d_row, d_col = iota((128, 128), 0), iota((128, 128), 1)
    same = (d_row // PLANE) == (d_col // PLANE)
    before = mm(there, flag(same & (d_row < d_col)))
    totals = mm(there, flag(same)).astype(jnp.bfloat16)
    earlier = mm(flag(iota((8, 8), 1) < iota((8, 8), 0)), totals)
    rank = before + earlier
    identity = flag(d_row == d_col)
    slot_cols = mm(identity, slots_t.astype(jnp.float32).astype(jnp.bfloat16), RIGHT)
    rank_cols = mm(identity, jnp.where(present, rank, 0.0).astype(jnp.bfloat16), RIGHT)
    away = (iota((128, 1), 0) // PLANE + PLANES - z) % PLANES
    z_slot = jnp.where(away == 0, 0, jnp.where(away <= PLANES // 2, 2 * away - 1, 2 * (PLANES - away)))
    plane_base = (CAPACITY * z_slot).astype(jnp.float32) + 1.0
    slot_lane = iota((1, n_slots), 1).astype(jnp.float32)
    found = jnp.zeros((128, n_slots), jnp.float32)
    for j in range(IMG_MAX):
        found = found + jnp.where(
            slot_cols[:, j : j + 1] == slot_lane, rank_cols[:, j : j + 1] + plane_base, 0.0
        )
    goes_to = jnp.sum(found, axis=0, keepdims=True) - 1.0
    pick1[...] = flag(iota((PLANES * CAPACITY, n_slots), 0).astype(jnp.float32) == goes_to)

    def by_document(entries, rows, per_document):
        step = iota((rows, 128), 0) // per_document
        row_doc = z * PLANE + ((px + step // 4) % 4) * 4 + (py + step % 4) % 4
        by_slot = mm(flag(iota((rows, 128), 1) == row_doc), entries.astype(jnp.bfloat16), RIGHT)
        chosen = iota((rows, IMG_MAX), 1) == iota((rows, IMG_MAX), 0) % IMG_MAX
        return jnp.sum(jnp.where(chosen, by_slot, 0.0), axis=1, keepdims=True)

    rows_o = PLANE * IMG_MAX
    slot_plus = jnp.where(present, (slots_t + 1).astype(jnp.float32), 0.0)
    rank_plus = jnp.where(present, rank + 1.0, 0.0)
    pick_own[...] = flag(iota((rows_o, n_slots), 1).astype(jnp.float32) == by_document(slot_plus, rows_o, IMG_MAX) - 1.0)

    lane = iota((1, HEAD_SIZE), 1)
    first_t = jnp.zeros((1, HEAD_SIZE), jnp.int32)
    last_t = jnp.zeros((1, HEAD_SIZE), jnp.int32)
    for j in range(IMG_MAX):
        first_t = jnp.where(lane == j, pos_ref[0, j], first_t)
        last_t = jnp.where(lane == j, end_ref[0, j], last_t)
    block = iota((4 * tokens, HEAD_SIZE), 0) // (2 * tokens)
    owner = jnp.where(block == 0, core, sibling)
    t_pos = owner * tokens + iota((4 * tokens, HEAD_SIZE), 0) % tokens
    attends = (lane < count_ref[0]) & (first_t <= t_pos) & (t_pos < last_t)
    q_tail[...] = flag(jnp.logical_not(attends))
    n_keys = k_tail.shape[0]
    k_tail[...] = jnp.where(
        iota((n_keys, HEAD_SIZE), 1) == iota((n_keys, HEAD_SIZE), 0) % IMG_MAX, MASKED, 0.0
    ).astype(jnp.bfloat16)

    def part_copy(i):
        total, got = ((sum_k, got_k), (sum_v, got_v))[i]
        return pltpu.make_async_remote_copy(
            src_ref=total.at[:, sib_half],
            dst_ref=got,
            send_sem=part_sems.at[0, i],
            recv_sem=part_sems.at[1, i],
            device_id=(doc, sibling),
            device_id_type=MESH,
        )

    for i in range(4):
        x_copy(i).wait()
    for n, (i, c) in enumerate(order):
        w, total = ((wk_v, sum_k), (wv_v, sum_v))[i]
        cols = pl.ds(c * piece, piece)
        w_copy(i, c).wait()
        if n + AHEAD < len(order):
            w_copy(*order[n + AHEAD]).start()
        elif n + AHEAD == len(order):
            q_copy.start()
        term = mm(x_v[:, cols], w[cols, :])
        total[...] = term if c == 0 else total[...] + term
        if (i, c) == (0, PIECES - 1):
            pl.semaphore_wait(barrier, PLANES - 1 + PLANE - 1 + 1)
            part_copy(0).start()
    part_copy(1).start()

    q_copy.wait()
    q_gain = qg_ref[...]
    half_width = QUERY_HEADS // 2 * HEAD_SIZE

    def norm_queries(n, carry):
        for u in range(4):
            i = n * 4 + u
            at = pl.multiple_of(i * HEAD_SIZE, HEAD_SIZE)
            own_cols = pl.ds(pl.multiple_of(core * half_width + at, HEAD_SIZE), HEAD_SIZE)
            sib_cols = pl.ds(pl.multiple_of(sibling * half_width + at, HEAD_SIZE), HEAD_SIZE)
            q_own[i] = head_norm(q_v[:, own_cols].astype(jnp.float32), q_gain).astype(jnp.bfloat16)
            q_send[i] = head_norm(q_v[:, sib_cols].astype(jnp.float32), q_gain).astype(jnp.bfloat16)
        return carry

    lax.fori_loop(0, QUERY_HEADS // 8, norm_queries, 0)
    q_exchange = pltpu.make_async_remote_copy(
        src_ref=q_send,
        dst_ref=q_sib,
        send_sem=q_sems.at[0],
        recv_sem=q_sems.at[1],
        device_id=(doc, sibling),
        device_id_type=MESH,
    )

    q_exchange.start()

    def hop1(s):
        return pltpu.make_async_remote_copy(
            src_ref=send1.at[s],
            dst_ref=recv1.at[s],
            send_sem=s1_sem.at[s],
            recv_sem=r1_sem.at[s],
            device_id=(z_to(s) * PLANE + p, core),
            device_id_type=MESH,
        )

    def hop2(k, i):
        return pltpu.make_async_remote_copy(
            src_ref=send2.at[k, i],
            dst_ref=recv2.at[k, i],
            send_sem=s2_sem.at[k],
            recv_sem=r2_sem.at[k],
            device_id=(z * PLANE + plane_to(i), core),
            device_id_type=MESH,
        )

    def await_group(ref, k, sem):
        part = ref.at[k, pl.ds(1, PLANE - 1)]
        pltpu.make_async_copy(part, part, sem.at[k]).wait()

    key_gain = kg_ref[...]
    part_copy(0).wait_recv()
    raw_k = sum_k[:, own_half] + got_k[...]
    keys_own = [head_norm(raw_k[:, h * HEAD_SIZE : (h + 1) * HEAD_SIZE], key_gain).astype(jnp.bfloat16) for h in range(2)]
    part_copy(1).wait_recv()
    raw_v = (sum_v[:, own_half] + got_v[...]).astype(jnp.bfloat16)
    kv_own = jnp.concatenate(keys_own + [raw_v], axis=1)
    packed = mm(pick1[...], kv_own).astype(jnp.bfloat16).reshape(PLANES, CAPACITY, 2 * half)
    for s in range(1, PLANES):
        send1[s] = packed[s]
    for s in range(1, 5):
        hop1(s).start()
    def hop_one(n, i):
        return pltpu.make_async_remote_copy(
            src_ref=send_one.at[n, i],
            dst_ref=recv_one.at[n, i],
            send_sem=so_sem.at[n],
            recv_sem=ro_sem.at[n],
            device_id=(z * PLANE + plane_to(i), core),
            device_id_type=MESH,
        )

    def send_single(n, rows):
        rows = rows.reshape(PLANE, IMG_MAX, 2 * half)
        rows = jnp.concatenate([rows[:, :, :half], rows[:, :, half:]], axis=1).astype(jnp.bfloat16)
        recv_one[n, 0] = rows[0]
        send_one[n, pl.ds(1, PLANE - 1)] = rows[1:]

        def body(i, carry):
            hop_one(n, PLANE - i).start()
            return carry

        lax.fori_loop(1, PLANE, body, 0)

    send_single(0, mm(pick_own[...], kv_own))
    for s in range(5, PLANES):
        hop1(s).start()
    pair = 2 * IMG_MAX
    rows_e, cols_e = PLANE * pair, 2 * CAPACITY
    row_rank = by_document(rank_plus, rows_e, pair)
    source = (iota((rows_e, 1), 0) // IMG_MAX) % 2
    row_target = jnp.where(row_rank > 0.0, row_rank - 1.0 + (CAPACITY * source).astype(jnp.float32), -1.0)
    expand_far[...] = flag(
        iota((rows_o, CAPACITY), 1).astype(jnp.float32) == by_document(rank_plus, rows_o, IMG_MAX) - 1.0
    )
    expand[...] = flag(iota((rows_e, cols_e), 1).astype(jnp.float32) == row_target)

    def expand_and_send(k):
        for s in (2 * k + 1, 2 * k + 2):
            hop1(s).wait_recv()
        rows = mm(expand[...], recv1[pl.ds(2 * k + 1, 2)].reshape(2 * CAPACITY, 2 * half)).astype(jnp.bfloat16)
        rows = rows.reshape(PLANE, pair, 2 * half)
        recv2[k, 0] = rows[0]
        send2[k, pl.ds(1, PLANE - 1)] = rows[1:]

        def body(i, carry):
            hop2(k, PLANE - i).start()
            return carry

        lax.fori_loop(1, PLANE, body, 0)

    ones = jnp.ones((n_keys, HEAD_SIZE), jnp.bfloat16)
    scale = 1.0 / math.sqrt(HEAD_SIZE)
    last = PLANES // 2 - 1

    blocks = GROUP
    per_head = blocks // 2

    def attend(k):
        if k < last:
            await_group(recv2, k, r2_sem)
        else:
            await_group(recv_one, 0, ro_sem)
            await_group(recv_one, 1, ro_sem)
            rows = recv_one[...].astype(jnp.float32)
            keys = rows[:, :, :IMG_MAX].reshape(n_keys, half)
            values = rows[:, :, IMG_MAX:].reshape(n_keys, half)
            joined = jnp.concatenate([keys, values], axis=1).astype(jnp.bfloat16)
            recv2[k] = joined.reshape(PLANE, pair, 2 * half)

        def keys_of(b):
            at = (b // per_head) * HEAD_SIZE
            rows = recv2[k, :, :, at : at + HEAD_SIZE].reshape(n_keys, HEAD_SIZE)
            return jnp.concatenate([rows, k_tail[...]], axis=1)

        def values_of(b):
            at = half + (b // per_head) * HEAD_SIZE
            rows = recv2[k, :, :, at : at + HEAD_SIZE].reshape(n_keys, HEAD_SIZE)
            return jnp.concatenate([rows, ones], axis=1)

        def scores_of(b):
            own = q_own[2 * b : 2 * b + 2].reshape(2 * tokens, HEAD_SIZE)
            sib = q_sib[2 * b : 2 * b + 2].reshape(2 * tokens, HEAD_SIZE)
            rows = jnp.concatenate([jnp.concatenate([own, sib], axis=0), q_tail[...]], axis=1)
            return mm(rows, keys_of(b), RIGHT)

        scores = scores_of(0)
        for b in range(blocks):
            weights = jnp.exp(scores * scale).astype(jnp.bfloat16)
            if b + 1 < blocks:
                scores = scores_of(b + 1)
            mixed = mm(weights, values_of(b))
            if k > 0:
                mixed = mixed + o_sum[b]
            if k < last:
                o_sum[b] = mixed
                continue
            total = mixed[:, HEAD_SIZE:]
            out = (mixed[:, :HEAD_SIZE] / jnp.where(total > 0.0, total, 1.0)).astype(jnp.bfloat16)
            for i in range(2):
                at = (2 * b + i) * HEAD_SIZE
                o_own[:, at : at + HEAD_SIZE] = out[i * tokens : (i + 1) * tokens]
                o_send[:, at : at + HEAD_SIZE] = out[(2 + i) * tokens : (3 + i) * tokens]
            if b % 2 == 1:
                o_copy(b // 2).start()
                own_copy(b // 2).start()

    quarters = 4
    out_width = width // 2 // quarters

    def out_at(of, h):
        return out_hbm.at[:, pl.ds(pl.multiple_of((of * quarters + h) * out_width, out_width), out_width)]

    def o_copy(h):
        return pltpu.make_async_remote_copy(
            src_ref=o_send.at[:, pl.ds(h * out_width, out_width)],
            dst_ref=out_at(core, h),
            send_sem=o_sems.at[0, h],
            recv_sem=o_sems.at[1, h],
            device_id=(doc, sibling),
            device_id_type=MESH,
        )

    def o_in(h):
        return pltpu.make_async_remote_copy(
            src_ref=o_send.at[:, pl.ds(h * out_width, out_width)],
            dst_ref=out_at(sibling, h),
            send_sem=o_sems.at[0, h],
            recv_sem=o_sems.at[1, h],
            device_id=(doc, sibling),
            device_id_type=MESH,
        )

    def own_copy(h):
        return pltpu.make_async_copy(o_own.at[:, pl.ds(h * out_width, out_width)], out_at(core, h), out_sem.at[h])

    expand_and_send(0)
    expand_and_send(1)
    q_exchange.wait_recv()
    expand_and_send(2)
    attend(0)
    hop1(PLANES - 1).wait_recv()
    send_single(1, mm(expand_far[...], recv1[PLANES - 1]))
    attend(1)
    attend(2)
    attend(3)

    for i in range(2):
        part_copy(i).wait_send()
    for s in range(1, PLANES):
        hop1(s).wait_send()
    for k in range(last):
        await_group(send2, k, s2_sem)
    await_group(send_one, 0, so_sem)
    await_group(send_one, 1, so_sem)
    q_exchange.wait_send()
    for h in range(quarters):
        o_copy(h).wait_send()
        own_copy(h).wait()
        o_in(h).wait_recv()


def packed_route(
    queries,
    vision,
    key_matrix,
    value_matrix,
    query_gain,
    key_gain,
    image_count,
    image_slot,
    image_pos,
    span_end,
):
    tokens, width = queries.shape
    n_slots = vision.shape[0]
    depth = vision.shape[2]
    two = 2 * HEAD_SIZE
    anywhere = pl.BlockSpec(memory_space=pl.ANY)
    smem = pl.BlockSpec(memory_space=pltpu.SMEM)
    bf16, f32 = jnp.bfloat16, jnp.float32
    dma = pltpu.SemaphoreType.DMA
    groups = PLANES // 2
    pair = 2 * IMG_MAX
    out = pl.pallas_call(
        fused_kernel,
        out_shape=jax.ShapeDtypeStruct((tokens, width), bf16),
        in_specs=[anywhere] * 6 + [smem, anywhere, smem, smem],
        out_specs=anywhere,
        scratch_shapes=[
            pltpu.VMEM((1, HEAD_SIZE), f32),
            pltpu.VMEM((1, HEAD_SIZE), f32),
            pltpu.VMEM((IMG_MAX, image_slot.shape[0]), jnp.int32),
            pltpu.VMEM((tokens, width), bf16),
            pltpu.VMEM((n_slots, depth), bf16),
            pltpu.VMEM(key_matrix.shape, bf16),
            pltpu.VMEM(value_matrix.shape, bf16),
            pltpu.VMEM((n_slots, 2 * two), f32),
            pltpu.VMEM((n_slots, 2 * two), f32),
            pltpu.VMEM((n_slots, two), f32),
            pltpu.VMEM((n_slots, two), f32),
            pltpu.VMEM((PLANES * CAPACITY, n_slots), bf16),
            pltpu.VMEM((PLANE * pair, 2 * CAPACITY), bf16),
            pltpu.VMEM((PLANE * IMG_MAX, n_slots), bf16),
            pltpu.VMEM((PLANE * IMG_MAX, CAPACITY), bf16),
            pltpu.VMEM((PLANES, CAPACITY, 2 * two), bf16),
            pltpu.VMEM((PLANES, CAPACITY, 2 * two), bf16),
            pltpu.VMEM((groups, PLANE, pair, 2 * two), bf16),
            pltpu.VMEM((groups, PLANE, pair, 2 * two), bf16),
            pltpu.VMEM((2, PLANE, pair, two), bf16),
            pltpu.VMEM((2, PLANE, pair, two), bf16),
            pltpu.VMEM((QUERY_HEADS // 2, tokens, HEAD_SIZE), bf16),
            pltpu.VMEM((QUERY_HEADS // 2, tokens, HEAD_SIZE), bf16),
            pltpu.VMEM((QUERY_HEADS // 2, tokens, HEAD_SIZE), bf16),
            pltpu.VMEM((4 * tokens, HEAD_SIZE), bf16),
            pltpu.VMEM((PLANE * pair, HEAD_SIZE), bf16),
            pltpu.VMEM((GROUP, 4 * tokens, two), f32),
            pltpu.VMEM((tokens, width // 2), bf16),
            pltpu.VMEM((tokens, width // 2), bf16),
            dma((8,)),
            dma((2, PIECES)),
            dma((4,)),
            dma((2, 2)),
            dma((2,)),
            dma((2, 4)),
            dma((PLANES,)),
            dma((PLANES,)),
            dma((groups,)),
            dma((groups,)),
            dma((2,)),
            dma((2,)),
        ],
        compiler_params=pltpu.CompilerParams(
            collective_id=0, has_side_effects=True, vmem_limit_bytes=56 * 1024 * 1024
        ),
        name="fused_cross_attention",
    )(
        queries,
        vision.reshape(n_slots, depth),
        key_matrix,
        value_matrix,
        query_gain.reshape(1, HEAD_SIZE),
        key_gain.reshape(1, HEAD_SIZE),
        image_count,
        image_slot.T,
        image_pos,
        span_end,
    )
    return out


def fits_kernel(slot_ref, fits_ref):
    same = (iota((128, 128), 0) // PLANE) == (iota((128, 128), 1) // PLANE)
    totals = mm(flag(slot_ref[...] >= 0), flag(same))
    crowded = jnp.max(jnp.sum(totals, axis=0, keepdims=True))
    fits_ref[0] = jnp.where(crowded <= CAPACITY, 1, 0)


def shards(*arrays):
    image_slot = arrays[7]
    fits = pl.pallas_call(
        fits_kernel,
        out_shape=jax.ShapeDtypeStruct((1,), jnp.int32),
        in_specs=[pl.BlockSpec(memory_space=pltpu.VMEM)],
        out_specs=pl.BlockSpec(memory_space=pltpu.SMEM),
        name="fits",
    )(image_slot.T)
    return lax.cond(fits[0] > 0, packed_route, general_route, *arrays)

def solution(mesh):
    in_specs = (
        P(("doc", "seq"), None),
        P(None, "doc", "seq"),
        P("seq", None),
        P("seq", None),
        P(),
        P(),
        P("doc"),
        P(),
        P("doc", None),
        P("doc", None),
    )
    out_specs = P(("doc", "seq"), None)
    return jax.shard_map(shards, mesh=mesh, in_specs=in_specs, out_specs=out_specs, check_vma=False)
```
